32 devices in a mesh: seq: 8 (over z, x), head: 4 (over y, core).
Axes of the slice: x: 2, y: 2, z: 4, core: 2. Of those that a mesh axis runs over, the one named last changes fastest.
Arguments:
- queries: bfloat16 [8192, 4096], P(('seq', 'head'))
- keys: bfloat16 [8192, 2048], P(('seq', 'head'))
- values: bfloat16 [8192, 2048], P(('seq', 'head')), may hold values from -6 to 6
- dout: bfloat16 [8192, 4096], P(('seq', 'head')), may hold values from -6 to 6
- doc_starts: int32 [8], replicated, may hold values from 0 to 8191, as said below
Outputs:
- dquery: bfloat16 [8192, 4096], P(('seq', 'head'))
- dkey: bfloat16 [8192, 2048], P(('seq', 'head'))
- dvalue: bfloat16 [8192, 2048], P(('seq', 'head'))
The draws below stay inside these ranges and needn't reach their ends.
Inputs may be any that keep to these rules, and one draw needn't show every extreme that they name: doc_starts[0] = 0, strictly increasing.
All inputs are finite; a program needn't handle non-finite values.
Results may differ from the reference program's by a relative error of at most 0.03.
Values may be sent and summed in bfloat16 or wider, within the bound.
No kernel may reach another device: no remote copies, remote signals or barrier semaphores. Data moves between devices by JAX's collectives and lax.ppermute only.
A program may use at most 128 MiB of HBM per device.

```python
import jax
import jax.numpy as jnp
from jax import lax

QUERY_HEADS = 32
KEY_VALUE_HEADS = 16
HEAD_SIZE = 128
WINDOW_LENGTH = 512
PACKED_TOKENS = 8192
DOCS = 8


def paired_draw(key):
    query_group = QUERY_HEADS // KEY_VALUE_HEADS
    query_random_key = jax.random.fold_in(key, 11)
    keys_random_key = jax.random.fold_in(key, 23)
    query_entries = jax.random.normal(query_random_key, (PACKED_TOKENS, KEY_VALUE_HEADS, query_group, HEAD_SIZE), jnp.float32)
    key_entries = jax.random.normal(keys_random_key, (PACKED_TOKENS, KEY_VALUE_HEADS, HEAD_SIZE), jnp.float32)
    return (query_entries.reshape(PACKED_TOKENS, QUERY_HEADS * HEAD_SIZE), key_entries.reshape(PACKED_TOKENS, KEY_VALUE_HEADS * HEAD_SIZE))


def draw_queries(key, part):
    return paired_draw(key)[0].astype(jnp.bfloat16)


def draw_keys(key, part):
    return paired_draw(key)[1].astype(jnp.bfloat16)


def draw_doc_starts(key, part):
    inner = jax.random.permutation(jax.random.fold_in(key, 5), PACKED_TOKENS - 1)[:DOCS - 1] + 1
    return jnp.concatenate([jnp.zeros((1,), jnp.int32), jnp.sort(inner.astype(jnp.int32))]).astype(jnp.int32)


def shard_levels(own_key, dims, shards, low, top_value):
    factor_of, own = 1.0, jax.random.fold_in(own_key, 6)
    for axis_at, parts in shards:
        draws = jnp.exp(jax.random.uniform(jax.random.fold_in(own, axis_at), (parts,), jnp.float32, low / len(shards), top_value / len(shards)))
        factor_of = factor_of * jnp.repeat(draws, dims[axis_at] // parts).reshape([-1 if axis == axis_at else 1 for axis in range(len(dims))])
    return factor_of


def noise(own_key, dims, width, most, shards=(), kind=jnp.bfloat16):
    drawn = jax.random.normal(own_key, dims, jnp.float32) * width
    if len(shards) > 0:
        drawn = shard_levels(own_key, dims, shards, -0.22, 0.18) * drawn
    return jnp.clip(drawn, min=-most, max=most).astype(kind)


def setup_inputs(seed: int = 0) -> dict:
    key_of = jax.random.split(jax.random.key(seed), 6)
    return {
        "queries": draw_queries(jax.random.fold_in(key_of[5], 71), 0),
        "keys": draw_keys(jax.random.fold_in(key_of[5], 71), 0),
        "values": noise(key_of[2], (PACKED_TOKENS, KEY_VALUE_HEADS * HEAD_SIZE), 1.0, 6.0, ((0, 32),)),
        "dout": noise(key_of[3], (PACKED_TOKENS, QUERY_HEADS * HEAD_SIZE), 1.0, 6.0, ((0, 32),)),
        "doc_starts": draw_doc_starts(jax.random.fold_in(key_of[5], 71), 0),
    }


scale_factor = 168.0 ** -0.5
negative = -1.0e30


def doc_ids(positions, doc_starts):
    return jnp.sum((doc_starts[None, :] <= positions[:, None]).astype(jnp.int32), axis=1) - 1


def allowed_pairs(query_pos, key_pos, doc_starts, limit, window):
    query_doc = doc_ids(query_pos, doc_starts)
    key_doc = doc_ids(key_pos, doc_starts)
    return ((key_pos[None, :] >= 0) & (key_pos[None, :] <= query_pos[:, None])
            & (query_pos[:, None] - key_pos[None, :] < window)
            & (query_doc[:, None] == key_doc[None, :]) & (query_pos[:, None] < limit))


def reference(queries, keys, values, dout, doc_starts):
    query_group = QUERY_HEADS // KEY_VALUE_HEADS
    blocks = PACKED_TOKENS // WINDOW_LENGTH
    query_four_axes = queries.reshape(PACKED_TOKENS, KEY_VALUE_HEADS, query_group, HEAD_SIZE)
    gradient_four_axes = dout.reshape(PACKED_TOKENS, KEY_VALUE_HEADS, query_group, HEAD_SIZE)
    padding_tokens = jnp.zeros((WINDOW_LENGTH, KEY_VALUE_HEADS, HEAD_SIZE), jnp.bfloat16)
    extended_keys = jnp.concatenate([padding_tokens, keys.reshape(PACKED_TOKENS, KEY_VALUE_HEADS, HEAD_SIZE)], axis=0)
    extended_values = jnp.concatenate([padding_tokens, values.reshape(PACKED_TOKENS, KEY_VALUE_HEADS, HEAD_SIZE)], axis=0)
    spread = jnp.arange(WINDOW_LENGTH, dtype=jnp.int32)
    double = jnp.arange(2 * WINDOW_LENGTH, dtype=jnp.int32)

    def one_block(blk):
        start = (blk * WINDOW_LENGTH).astype(jnp.int32)
        q_blk = lax.dynamic_slice_in_dim(query_four_axes, start, WINDOW_LENGTH, 0).astype(jnp.float32)
        g_blk = lax.dynamic_slice_in_dim(gradient_four_axes, start, WINDOW_LENGTH, 0).astype(jnp.float32)
        k_blk = lax.dynamic_slice_in_dim(extended_keys, start, 2 * WINDOW_LENGTH, 0).astype(jnp.float32)
        v_blk = lax.dynamic_slice_in_dim(extended_values, start, 2 * WINDOW_LENGTH, 0).astype(jnp.float32)
        allowed = allowed_pairs(start + spread, start - WINDOW_LENGTH + double, doc_starts, PACKED_TOKENS, WINDOW_LENGTH)
        scores = jnp.einsum("qhgd,khd->hgqk", q_blk, k_blk) * scale_factor
        masked = jnp.where(allowed, scores, negative)
        peak = jnp.max(masked, axis=-1, keepdims=True)
        total = jnp.sum(jnp.exp(masked - peak), axis=-1, keepdims=True)
        log_sum = peak + jnp.log(total)
        probs = jnp.exp(masked - log_sum)
        probs_low = probs.astype(jnp.bfloat16)
        output = jnp.einsum("hgqk,khd->qhgd", probs_low.astype(jnp.float32), v_blk).astype(jnp.bfloat16)
        output = lax.optimization_barrier(output)
        delta = jnp.sum(g_blk * output.astype(jnp.float32), axis=-1)
        delta = jnp.transpose(delta, (1, 2, 0))[..., None]
        dprobs = jnp.einsum("qhgd,khd->hgqk", g_blk, v_blk)
        dscores = (probs * (dprobs - delta) * scale_factor).astype(jnp.bfloat16).astype(jnp.float32)
        dq_blk = jnp.einsum("hgqk,khd->qhgd", dscores, k_blk).astype(jnp.bfloat16)
        dk_blk = jnp.einsum("hgqk,qhgd->khd", dscores, q_blk)
        dv_blk = jnp.einsum("hgqk,qhgd->khd", probs_low.astype(jnp.float32), g_blk)
        return dq_blk, dk_blk, dv_blk

    dq_all, dk_all, dv_all = lax.map(one_block, jnp.arange(blocks, dtype=jnp.int32))
    tail_tokens = jnp.zeros((1, WINDOW_LENGTH, KEY_VALUE_HEADS, HEAD_SIZE), jnp.float32)
    key_gradient_total = dk_all[:, WINDOW_LENGTH:] + jnp.concatenate([dk_all[1:, :WINDOW_LENGTH], tail_tokens], axis=0)
    value_gradient_total = dv_all[:, WINDOW_LENGTH:] + jnp.concatenate([dv_all[1:, :WINDOW_LENGTH], tail_tokens], axis=0)
    dquery = dq_all.reshape(PACKED_TOKENS, QUERY_HEADS * HEAD_SIZE)
    dkey = key_gradient_total.reshape(PACKED_TOKENS, KEY_VALUE_HEADS * HEAD_SIZE).astype(jnp.bfloat16)
    dvalue = value_gradient_total.reshape(PACKED_TOKENS, KEY_VALUE_HEADS * HEAD_SIZE).astype(jnp.bfloat16)
    return (dquery, dkey, dvalue)
```

```python
import functools
import math

import jax
import jax.numpy as jnp
from jax import lax
from jax.experimental import pallas as pl
from jax.experimental.pallas import tpu as pltpu
from jax.sharding import PartitionSpec as P

HEAD_SIZE = 128
WINDOW_LENGTH = 512
AXES = ("seq", "head")
GROUPS = (6, 6, 4)
STEP = 2
UNIT = 128
STRIP = 32
VMEM_LIMIT = 16 * 1024 * 1024


scale_factor = 168.0 ** (-0.5)
log2_scale = scale_factor * math.log2(math.e)
negative = -1e30


def shifted(x, by, devices):
    pairs = [(i, i + by) for i in range(devices) if 0 <= i + by < devices]
    return lax.ppermute(x, AXES, pairs)


def swapped(x, devices):
    return lax.ppermute(x, AXES, [(i, i ^ 1) for i in range(devices)])


def to_odd(x, devices):
    return lax.ppermute(x, AXES, [(i, i + 1) for i in range(0, devices, 2)])


def to_even(x, devices):
    return lax.ppermute(x, AXES, [(i + 1, i) for i in range(0, devices, 2)])


def after(x, *others):
    return lax.optimization_barrier((x, *others))[0]


def dot_rows(left, right):
    return lax.dot_general(
        left, right, (((1,), (1,)), ((), ())), preferred_element_type=jnp.float32
    )


def dot_cols(left, right):
    return lax.dot_general(
        left, right, (((0,), (0,)), ((), ())), preferred_element_type=jnp.float32
    )


def dot(left, right):
    return jnp.dot(left, right, preferred_element_type=jnp.float32)


def merged(x, unit, pick_ref, at):
    if at >= unit:
        return x[at : at + STRIP]
    last = x.shape[0] - unit + at
    own = pick_ref[at : at + STRIP] > 0.5
    return jnp.where(own, x[last : last + STRIP], x[at : at + STRIP])


def spread(strips, unit, tri):
    edge = jnp.concatenate(strips[: unit // STRIP], axis=0)
    own = edge * tri
    return jnp.concatenate([edge - own] + strips[unit // STRIP :] + [own], axis=0)


def weigh(scores, dprobs, unit, bounds, pick_ref, tri):
    strips = range(0, scores.shape[0] - unit, STRIP)
    kept, peak = [], None
    for at in strips:
        s = jnp.minimum(merged(scores, unit, pick_ref, at), bounds[at : at + STRIP])
        kept.append(s)
        peak = s if peak is None else jnp.maximum(peak, s)
    peak = jnp.max(peak, axis=0, keepdims=True)
    low, dps = [], []
    total, weighted = 0.0, 0.0
    for at, s in zip(strips, kept):
        e = jnp.exp2((s - peak) * log2_scale)
        dp = merged(dprobs, unit, pick_ref, at)
        total = total + e
        weighted = weighted + e * dp
        low.append(e.astype(jnp.bfloat16))
        dps.append(dp)
    inverse = 1.0 / jnp.sum(total, axis=0, keepdims=True)
    delta = jnp.sum(weighted, axis=0, keepdims=True) * inverse
    ds = [e * (dp - delta).astype(jnp.bfloat16) for e, dp in zip(low, dps)]
    return spread(low, unit, tri), spread(ds, unit, tri), inverse


def products(q, g, k, low, ds, inverse):
    by_row = jnp.transpose(jnp.broadcast_to(inverse, (HEAD_SIZE, q.shape[0])))
    g_scaled = (g.astype(jnp.float32) * by_row).astype(jnp.bfloat16)
    q_scaled = (q.astype(jnp.float32) * (by_row * scale_factor)).astype(jnp.bfloat16)
    dv = dot(low, g_scaled)
    dk = dot(ds, q_scaled)
    dq = jnp.transpose(dot_cols(k, ds) * (inverse * scale_factor)).astype(jnp.bfloat16)
    return dq, dk, dv


def kernel(rows, back, group, split, pieces, base_ref, starts_ref, q_ref, g_ref, k_ref, v_ref, *refs):
    pairs = [refs[2 * j : 2 * j + 2] for j in range(back + split)]
    outs = refs[len(refs) - (back + 1 + pieces) - 3 : len(refs) - 3]
    bound_ref, pick_ref, tri_ref = refs[-3:]
    dq_ref, own_ref, near_refs, far_refs = outs[0], outs[1], outs[2 : 2 + pieces], outs[2 + pieces :]
    unit = min(UNIT, rows)
    units = rows // unit
    columns = group * unit
    span = back * rows

    @pl.when(pl.program_id(0) == 0)
    def _():
        col = lax.broadcasted_iota(jnp.int32, (unit, columns), 1) % unit
        row = lax.broadcasted_iota(jnp.int32, (unit, columns), 0)
        own = row <= col
        pick_ref[...] = own.astype(jnp.float32)
        tri_ref[...] = pick_ref[...].astype(jnp.bfloat16)
        for u in range(units):
            base = base_ref[0] + u * unit
            pos = base + col[:1]
            start = jnp.zeros_like(pos)
            for doc in range(starts_ref.shape[0]):
                at = starts_ref[doc]
                start = jnp.where(pos >= at, at, start)
            start = jnp.broadcast_to(start, (unit, columns))
            for at in range(0, span, unit):
                key_pos = base - span + at + row
                if at == 0:
                    key_pos = jnp.where(own, key_pos + span, key_pos)
                bound_ref[u, at : at + unit] = jnp.where(key_pos >= start, jnp.inf, negative)

    tri = tri_ref[...]
    heads = range(k_ref.shape[1] // HEAD_SIZE)
    works = []
    for h in heads:
        at = slice(h * HEAD_SIZE, (h + 1) * HEAD_SIZE)

        def gathered(own, half):
            blocks = [pair[half][:, at] for pair in pairs]
            if split:
                blocks[:2] = [blocks[0] + blocks[1]]
            return jnp.concatenate(blocks[::-1] + [own[:, at]], axis=0)

        k_all = gathered(k_ref, 0)
        v_all = gathered(v_ref, 1)
        for u in range(units):
            of_rows = slice(u * unit, (u + 1) * unit)
            wide = [
                slice((h * group + m) * HEAD_SIZE, (h * group + m + 1) * HEAD_SIZE)
                for m in range(group)
            ]
            q = jnp.concatenate([q_ref[of_rows, w] for w in wide], axis=0)
            g = jnp.concatenate([g_ref[of_rows, w] for w in wide], axis=0)
            seen = slice(u * unit, u * unit + span + unit)
            works.append((h, u, of_rows, wide, q, g, k_all[seen], v_all[seen]))

    def begin(work):
        h, u, of_rows, wide, q, g, k, v = work
        return dot_rows(k, q), dot_rows(v, g)

    sums = {}
    ahead = begin(works[0])
    for i, work in enumerate(works):
        h, u, of_rows, wide, q, g, k, v = work
        scores, dprobs = ahead
        if i + 1 < len(works):
            ahead = begin(works[i + 1])
        low, ds, inverse = weigh(scores, dprobs, unit, bound_ref.at[u], pick_ref, tri)
        dq, dk, dv = products(q, g, k, low, ds, inverse)
        for m, w in enumerate(wide):
            dq_ref[of_rows, w] = dq[m * unit : (m + 1) * unit]
        for name, term in (("k", dk), ("v", dv)):
            for j in range((span + unit) // unit):
                key = (name, u + j)
                piece = term[j * unit : (j + 1) * unit]
                sums[key] = piece if key not in sums else sums[key] + piece
        if u + 1 < units:
            continue
        at = slice(h * HEAD_SIZE, (h + 1) * HEAD_SIZE)
        order = [[x] for x in far_refs[::-1]] + [near_refs, [own_ref]]
        for j, arrays in enumerate(order):
            height = 2 * rows // len(arrays)
            for name, below in (("k", 0), ("v", rows)):
                for of_unit in range(units):
                    piece, to = divmod(below + of_unit * unit, height)
                    total = sums[(name, j * units + of_unit)].astype(jnp.bfloat16)
                    arrays[piece][to : to + unit, at] = total
        sums = {}


def attend(
    base, doc_starts, queries, dout, keys, values, near, others, first, heads, buffer, pieces
):
    rows, width = keys.shape
    back = 1 + len(others)
    group = queries.shape[1] // width
    step = STEP * HEAD_SIZE
    unit = min(UNIT, rows)

    def part(height, wide, offset, row=0):
        return pl.BlockSpec((height, wide), lambda i: (row, offset // STEP + i))

    wide = part(rows, group * step, first)
    narrow = part(rows, step, first)
    smem = pl.BlockSpec(memory_space=pltpu.SMEM)
    operands = [base, doc_starts, queries, dout, keys, values]
    in_specs = [smem, smem, wide, wide, narrow, narrow]
    for pair in near + others:
        operands += [pair[0], pair[-1]]
        in_specs += [part(rows, step, 0), part(rows, step, 0, 2 - len(pair))]
    if len(near) == 2:
        operands[6:] = [pltpu.with_memory_space_constraint(x, pltpu.VMEM) for x in operands[6:]]
    aliases = {}
    if buffer is not None:
        aliases = {len(operands): 0}
        operands.append(buffer)
        in_specs.append(pl.BlockSpec(memory_space=pl.ANY))
    whole = (2 * rows, heads * HEAD_SIZE)
    outs = [whole] + [(2 * rows // pieces, heads * HEAD_SIZE)] * pieces + [whole] * (back - 1)
    outs = [queries.shape] + outs
    return pl.pallas_call(
        functools.partial(kernel, rows, back, group, len(near) == 2, pieces),
        grid=(heads // STEP,),
        in_specs=in_specs,
        out_specs=[wide] + [part(shape[0], step, 0) for shape in outs[1:]],
        out_shape=[jax.ShapeDtypeStruct(outs[0], jnp.bfloat16)]
        + [pltpu.VMEM(shape, jnp.bfloat16) for shape in outs[1:]],
        scratch_shapes=[
            pltpu.VMEM((rows // unit, back * rows, group * unit), jnp.float32),
            pltpu.VMEM((unit, group * unit), jnp.float32),
            pltpu.VMEM((unit, group * unit), jnp.bfloat16),
        ],
        input_output_aliases=aliases,
        compiler_params=pltpu.CompilerParams(vmem_limit_bytes=VMEM_LIMIT),
        cost_estimate=pl.CostEstimate(flops=1, bytes_accessed=1, transcendentals=0),
        name="attend",
    )(*operands)


def pack_kernel(first, k_ref, v_ref, *refs):
    outs, sems = refs[:-1], refs[-1]
    rows, wide = k_ref.shape[0], outs[0].shape[1]
    columns = pl.ds(first * HEAD_SIZE, wide)
    copies = []
    for i, ref in enumerate((k_ref, v_ref)):
        place = outs[i] if len(outs) == 2 else outs[0].at[pl.ds(i * rows, rows)]
        copies.append(pltpu.make_async_copy(ref.at[:, columns], place, sems.at[i]))
        copies[-1].start()
    for copy in copies:
        copy.wait()


def pack(keys, values, first, heads, arrays):
    rows, wide = keys.shape[0], heads * HEAD_SIZE
    keys, values = (pltpu.with_memory_space_constraint(x, pltpu.HBM) for x in (keys, values))
    shape = (2 * rows // arrays, wide)
    return pl.pallas_call(
        functools.partial(pack_kernel, first),
        in_specs=[pl.BlockSpec(memory_space=pl.ANY)] * 2,
        out_specs=[pl.BlockSpec(memory_space=pltpu.VMEM)] * arrays,
        out_shape=[pltpu.VMEM(shape, keys.dtype)] * arrays,
        scratch_shapes=[pltpu.SemaphoreType.DMA((2,))],
        compiler_params=pltpu.CompilerParams(vmem_limit_bytes=4 * 1024 * 1024),
        name="pack",
    )(keys, values)


def finish_kernel(odd_ref, own_ref, back_ref, home_ref, *refs):
    dk_ref, dv_ref = refs[-2:]
    rows = dk_ref.shape[0]
    back = back_ref[...].astype(jnp.float32)
    total = own_ref[...].astype(jnp.float32) + jnp.where(odd_ref[0] == 1, 0.0, back)
    total = total + home_ref[...].astype(jnp.float32)
    dk_ref[...] = total[:rows].astype(dk_ref.dtype)
    dv_ref[...] = total[rows:].astype(dv_ref.dtype)


def finish(odd, own, back, home, start, heads, width, buffers):
    rows, wide = own.shape[0] // 2, STEP * HEAD_SIZE
    operands = [odd] + [
        pltpu.with_memory_space_constraint(x, pltpu.VMEM) for x in (own, back, home)
    ]
    in_specs = [pl.BlockSpec(memory_space=pltpu.SMEM)]
    in_specs += [pl.BlockSpec((2 * rows, wide), lambda i: (0, i))] * 3
    aliases = {}
    if buffers is not None:
        aliases = {len(operands): 0, len(operands) + 1: 1}
        operands += buffers
        in_specs += [pl.BlockSpec(memory_space=pl.ANY)] * 2
    return pl.pallas_call(
        finish_kernel,
        grid=(heads // STEP,),
        in_specs=in_specs,
        out_specs=[pl.BlockSpec((rows, wide), lambda i: (0, start // STEP + i))] * 2,
        out_shape=[pltpu.HBM((rows, width), jnp.bfloat16)] * 2,
        input_output_aliases=aliases,
        compiler_params=pltpu.CompilerParams(vmem_limit_bytes=4 * 1024 * 1024),
        cost_estimate=pl.CostEstimate(flops=1, bytes_accessed=1, transcendentals=0),
        name="finish",
    )(*operands)


def shards(queries, keys, values, dout, doc_starts):
    rows, width = keys.shape
    kv_heads = width // HEAD_SIZE
    back = WINDOW_LENGTH // rows
    devices = lax.axis_size("seq") * lax.axis_size("head")
    index = lax.axis_index("seq") * lax.axis_size("head") + lax.axis_index("head")
    base = (index * rows).astype(jnp.int32).reshape(1)
    if back != 2 or lax.axis_size("head") % 2 != 0:
        both = jnp.concatenate([keys, values], axis=0)
        halos = [shifted(both, j, devices) for j in range(1, back + 1)]
        dquery, own, *sent = attend(
            base, doc_starts, queries, dout, keys, values, [[halos[0]]], [[x] for x in halos[1:]], 0,
            kv_heads, None, 1,
        )
        total = own.astype(jnp.float32)
        for j in range(back):
            total = total + shifted(sent[j], -(j + 1), devices).astype(jnp.float32)
        total = total.astype(jnp.bfloat16)
        return (dquery, total[:rows], total[rows:])

    odd = (index % 2).astype(jnp.int32).reshape(1)
    keys, values, base, odd = lax.optimization_barrier((keys, values, base, odd))
    starts = [sum(GROUPS[:c]) for c in range(len(GROUPS))]
    packed = [pack(keys, values, start, heads, 1)[0] for start, heads in zip(starts, GROUPS)]
    far = [shifted(x, 2, devices) for x in packed]
    early = [to_odd(x, devices) for x in packed]

    def work(start, heads, received, own_near, dquery):
        near = to_even(received, devices)
        dquery, own, to_near, to_far = attend(
            base, doc_starts, queries, dout, keys, values, [[near], [own_near]], [[received]],
            start, heads, dquery, 1,
        )
        returned = swapped(to_near, devices)
        extra = jnp.where(odd[0] == 1, returned.astype(jnp.float32), 0.0)
        send = (to_far.astype(jnp.float32) + extra).astype(jnp.bfloat16)
        return dquery, own, returned, send

    always = (doc_starts[0] | 1) != 0
    dquery, homes, kept = None, [], []
    for start, heads, received, own_near in zip(starts, GROUPS, far, early):
        def skip(received, own_near, dquery):
            zeros = jnp.zeros_like(received)
            return jnp.zeros_like(queries) if dquery is None else dquery, zeros, zeros, zeros

        dquery, own, returned, send = lax.cond(
            always, functools.partial(work, start, heads), skip, received, own_near, dquery
        )
        homes.append(shifted(send, -2, devices))
        kept.append((own, returned))
    grads = None
    for start, heads, home, (own, returned) in zip(starts, GROUPS, homes, kept):
        grads = finish(odd, own, returned, home, start, heads, width, grads)
    dkey, dvalue = grads
    return (dquery, dkey, dvalue)


def solution(mesh):
    spec = P(AXES, None)
    return jax.shard_map(
        shards,
        mesh=mesh,
        in_specs=(spec, spec, spec, spec, P()),
        out_specs=(spec, spec, spec),
        check_vma=False,
    )
```

```python
import functools
import math

import jax
import jax.numpy as jnp
from jax import lax
from jax.experimental import pallas as pl
from jax.experimental.pallas import tpu as pltpu
from jax.sharding import PartitionSpec as P

HEAD_SIZE = 128
WINDOW_LENGTH = 512
AXES = ("seq", "head")
GROUPS = ((8,), (4, 4))
STEP = 2
UNIT = 128
STRIP = 32
VMEM_LIMIT = 16 * 1024 * 1024


scale_factor = 168.0 ** (-0.5)
log2_scale = scale_factor * math.log2(math.e)
negative = -1e30


def device_index():
    return lax.axis_index("seq") * lax.axis_size("head") + lax.axis_index("head")


def shifted(x, by, devices):
    pairs = [(i, i + by) for i in range(devices) if 0 <= i + by < devices]
    return lax.ppermute(x, AXES, pairs)


def swapped(x, devices):
    return lax.ppermute(x, AXES, [(i, i ^ 1) for i in range(devices)])


def to_odd(x, devices):
    return lax.ppermute(x, AXES, [(i, i + 1) for i in range(0, devices, 2)])


def to_even(x, devices):
    return lax.ppermute(x, AXES, [(i + 1, i) for i in range(0, devices, 2)])


def after(x, *others):
    return lax.optimization_barrier((x, *others))[0]


def dot_rows(left, right):
    return lax.dot_general(
        left, right, (((1,), (1,)), ((), ())), preferred_element_type=jnp.float32
    )


def dot_cols(left, right):
    return lax.dot_general(
        left, right, (((0,), (0,)), ((), ())), preferred_element_type=jnp.float32
    )


def dot(left, right):
    return jnp.dot(left, right, preferred_element_type=jnp.float32)


def merged(x, unit, pick_ref, at):
    if at >= unit:
        return x[at : at + STRIP]
    last = x.shape[0] - unit + at
    own = pick_ref[at : at + STRIP] > 0.5
    return jnp.where(own, x[last : last + STRIP], x[at : at + STRIP])


def spread(strips, unit, tri):
    edge = jnp.concatenate(strips[: unit // STRIP], axis=0)
    own = edge * tri
    return jnp.concatenate([edge - own] + strips[unit // STRIP :] + [own], axis=0)


def weigh(scores, dprobs, unit, bounds, pick_ref, tri):
    strips = range(0, scores.shape[0] - unit, STRIP)
    kept, peak = [], None
    for at in strips:
        s = jnp.minimum(merged(scores, unit, pick_ref, at), bounds[at : at + STRIP])
        kept.append(s)
        peak = s if peak is None else jnp.maximum(peak, s)
    peak = jnp.max(peak, axis=0, keepdims=True)
    low, dps = [], []
    total, weighted = 0.0, 0.0
    for at, s in zip(strips, kept):
        e = jnp.exp2((s - peak) * log2_scale)
        dp = merged(dprobs, unit, pick_ref, at)
        total = total + e
        weighted = weighted + e * dp
        low.append(e.astype(jnp.bfloat16))
        dps.append(dp)
    inverse = 1.0 / jnp.sum(total, axis=0, keepdims=True)
    delta = jnp.sum(weighted, axis=0, keepdims=True) * inverse
    ds = [e * (dp - delta).astype(jnp.bfloat16) for e, dp in zip(low, dps)]
    return spread(low, unit, tri), spread(ds, unit, tri), inverse


def products(q, g, k, low, ds, inverse):
    by_row = jnp.transpose(jnp.broadcast_to(inverse, (HEAD_SIZE, q.shape[0])))
    g_scaled = (g.astype(jnp.float32) * by_row).astype(jnp.bfloat16)
    q_scaled = (q.astype(jnp.float32) * (by_row * scale_factor)).astype(jnp.bfloat16)
    dv = dot(low, g_scaled)
    dk = dot(ds, q_scaled)
    dq = jnp.transpose(dot_cols(k, ds) * (inverse * scale_factor)).astype(jnp.bfloat16)
    return dq, dk, dv


def kernel(rows, back, group, split, pieces, starts_ref, q_ref, g_ref, k_ref, v_ref, *refs):
    pairs = [refs[2 * j : 2 * j + 2] for j in range(back + split)]
    outs = refs[len(refs) - (back + 1 + pieces) - 3 : len(refs) - 3]
    bound_ref, pick_ref, tri_ref = refs[-3:]
    dq_ref, own_ref, near_refs, far_refs = outs[0], outs[1], outs[2 : 2 + pieces], outs[2 + pieces :]
    unit = min(UNIT, rows)
    units = rows // unit
    columns = group * unit
    span = back * rows

    @pl.when(pl.program_id(0) == 0)
    def _():
        col = lax.broadcasted_iota(jnp.int32, (unit, columns), 1) % unit
        row = lax.broadcasted_iota(jnp.int32, (unit, columns), 0)
        own = row <= col
        pick_ref[...] = own.astype(jnp.float32)
        tri_ref[...] = pick_ref[...].astype(jnp.bfloat16)
        for u in range(units):
            base = device_index() * rows + u * unit
            pos = base + col[:1]
            start = jnp.zeros_like(pos)
            for doc in range(starts_ref.shape[0]):
                at = starts_ref[doc]
                start = jnp.where(pos >= at, at, start)
            start = jnp.broadcast_to(start, (unit, columns))
            for at in range(0, span, unit):
                key_pos = base - span + at + row
                if at == 0:
                    key_pos = jnp.where(own, key_pos + span, key_pos)
                bound_ref[u, at : at + unit] = jnp.where(key_pos >= start, jnp.inf, negative)

    tri = tri_ref[...]
    heads = range(k_ref.shape[1] // HEAD_SIZE)
    works = []
    for h in heads:
        at = slice(h * HEAD_SIZE, (h + 1) * HEAD_SIZE)

        def gathered(own, half):
            blocks = [pair[half][:, at] for pair in pairs]
            if split:
                blocks[:2] = [blocks[0] + blocks[1]]
            return jnp.concatenate(blocks[::-1] + [own[:, at]], axis=0)

        k_all = gathered(k_ref, 0)
        v_all = gathered(v_ref, 1)
        for u in range(units):
            of_rows = slice(u * unit, (u + 1) * unit)
            wide = [
                slice((h * group + m) * HEAD_SIZE, (h * group + m + 1) * HEAD_SIZE)
                for m in range(group)
            ]
            q = jnp.concatenate([q_ref[of_rows, w] for w in wide], axis=0)
            g = jnp.concatenate([g_ref[of_rows, w] for w in wide], axis=0)
            seen = slice(u * unit, u * unit + span + unit)
            works.append((h, u, of_rows, wide, q, g, k_all[seen], v_all[seen]))

    def begin(work):
        h, u, of_rows, wide, q, g, k, v = work
        return dot_rows(k, q), dot_rows(v, g)

    sums = {}
    ahead = begin(works[0])
    for i, work in enumerate(works):
        h, u, of_rows, wide, q, g, k, v = work
        scores, dprobs = ahead
        if i + 1 < len(works):
            ahead = begin(works[i + 1])
        low, ds, inverse = weigh(scores, dprobs, unit, bound_ref.at[u], pick_ref, tri)
        dq, dk, dv = products(q, g, k, low, ds, inverse)
        for m, w in enumerate(wide):
            dq_ref[of_rows, w] = dq[m * unit : (m + 1) * unit]
        for name, term in (("k", dk), ("v", dv)):
            for j in range((span + unit) // unit):
                key = (name, u + j)
                piece = term[j * unit : (j + 1) * unit]
                sums[key] = piece if key not in sums else sums[key] + piece
        if u + 1 < units:
            continue
        at = slice(h * HEAD_SIZE, (h + 1) * HEAD_SIZE)
        order = [[x] for x in far_refs[::-1]] + [near_refs, [own_ref]]
        for j, arrays in enumerate(order):
            height = 2 * rows // len(arrays)
            for name, below in (("k", 0), ("v", rows)):
                for of_unit in range(units):
                    piece, to = divmod(below + of_unit * unit, height)
                    total = sums[(name, j * units + of_unit)].astype(jnp.bfloat16)
                    arrays[piece][to : to + unit, at] = total
        sums = {}


def attend(
    doc_starts, queries, dout, keys, values, near, others, start, first, heads, buffer, pieces
):
    rows, width = keys.shape
    back = 1 + len(others)
    group = queries.shape[1] // width
    step = STEP * HEAD_SIZE
    unit = min(UNIT, rows)

    def part(height, wide, offset, row=0):
        return pl.BlockSpec((height, wide), lambda i: (row, offset // STEP + i))

    wide = part(rows, group * step, first)
    narrow = part(rows, step, first)
    smem = pl.BlockSpec(memory_space=pltpu.SMEM)
    operands = [doc_starts, queries, dout, keys, values]
    in_specs = [smem, wide, wide, narrow, narrow]
    for pair in near + others:
        operands += [pair[0], pair[-1]]
        in_specs += [part(rows, step, first - start, row) for row in (0, 2 - len(pair))]
    if len(near) == 2:
        operands[5:] = [pltpu.with_memory_space_constraint(x, pltpu.VMEM) for x in operands[5:]]
    aliases = {}
    if buffer is not None:
        aliases = {len(operands): 0}
        operands.append(buffer)
        in_specs.append(pl.BlockSpec(memory_space=pl.ANY))
    whole = (2 * rows, heads * HEAD_SIZE)
    outs = [whole] + [(2 * rows // pieces, heads * HEAD_SIZE)] * pieces + [whole] * (back - 1)
    outs = [queries.shape] + outs
    return pl.pallas_call(
        functools.partial(kernel, rows, back, group, len(near) == 2, pieces),
        grid=(heads // STEP,),
        in_specs=in_specs,
        out_specs=[wide] + [part(shape[0], step, 0) for shape in outs[1:]],
        out_shape=[jax.ShapeDtypeStruct(outs[0], jnp.bfloat16)]
        + [pltpu.VMEM(shape, jnp.bfloat16) for shape in outs[1:]],
        scratch_shapes=[
            pltpu.VMEM((rows // unit, back * rows, group * unit), jnp.float32),
            pltpu.VMEM((unit, group * unit), jnp.float32),
            pltpu.VMEM((unit, group * unit), jnp.bfloat16),
        ],
        input_output_aliases=aliases,
        compiler_params=pltpu.CompilerParams(vmem_limit_bytes=VMEM_LIMIT),
        cost_estimate=pl.CostEstimate(flops=1, bytes_accessed=1, transcendentals=0),
        name="attend",
    )(*operands)


def pack_kernel(first, k_ref, v_ref, *refs):
    outs, sems = refs[:-1], refs[-1]
    rows, wide = k_ref.shape[0], outs[0].shape[1]
    columns = pl.ds(first * HEAD_SIZE, wide)
    copies = []
    for i, ref in enumerate((k_ref, v_ref)):
        place = outs[i] if len(outs) == 2 else outs[0].at[pl.ds(i * rows, rows)]
        copies.append(pltpu.make_async_copy(ref.at[:, columns], place, sems.at[i]))
        copies[-1].start()
    for copy in copies:
        copy.wait()


def pack(keys, values, first, heads, arrays):
    rows, wide = keys.shape[0], heads * HEAD_SIZE
    keys, values = (pltpu.with_memory_space_constraint(x, pltpu.HBM) for x in (keys, values))
    shape = (2 * rows // arrays, wide)
    return pl.pallas_call(
        functools.partial(pack_kernel, first),
        in_specs=[pl.BlockSpec(memory_space=pl.ANY)] * 2,
        out_specs=[pl.BlockSpec(memory_space=pltpu.VMEM)] * arrays,
        out_shape=[pltpu.VMEM(shape, keys.dtype)] * arrays,
        scratch_shapes=[pltpu.SemaphoreType.DMA((2,))],
        compiler_params=pltpu.CompilerParams(vmem_limit_bytes=4 * 1024 * 1024),
        name="pack",
    )(keys, values)


SMALL = pltpu.CompilerParams(vmem_limit_bytes=6 * 1024 * 1024)
FREE = pl.CostEstimate(flops=1, bytes_accessed=1, transcendentals=0)


def in_vmem(*arrays):
    return [pltpu.with_memory_space_constraint(x, pltpu.VMEM) for x in arrays]


def merge_kernel(far_ref, own_ref, back_ref, send_ref, kept_ref):
    odd = device_index() % 2 == 1

    @pl.when(odd)
    def _():
        total = far_ref[...].astype(jnp.float32) + back_ref[...].astype(jnp.float32)
        send_ref[...] = total.astype(send_ref.dtype)
        kept_ref[...] = own_ref[...]

    @pl.when(jnp.logical_not(odd))
    def _():
        send_ref[...] = far_ref[...]
        total = own_ref[...].astype(jnp.float32) + back_ref[...].astype(jnp.float32)
        kept_ref[...] = total.astype(kept_ref.dtype)


def merge(far, own, back):
    whole = pl.BlockSpec(memory_space=pltpu.VMEM)
    return pl.pallas_call(
        merge_kernel,
        in_specs=[whole] * 3,
        out_specs=[whole] * 2,
        out_shape=[pltpu.VMEM(far.shape, far.dtype)] * 2,
        compiler_params=SMALL,
        cost_estimate=FREE,
        name="merge",
    )(*in_vmem(far, own, back))


def finish_kernel(first, kept_ref, home_ref, *refs):
    outs, total_ref, sems = refs[-4:-2], refs[-2], refs[-1]
    rows, wide = kept_ref.shape[0] // 2, kept_ref.shape[1]
    copies = []
    for i, out in enumerate(outs):
        half = slice(i * rows, (i + 1) * rows)
        total = kept_ref[half].astype(jnp.float32) + home_ref[half].astype(jnp.float32)
        total_ref[half] = total.astype(total_ref.dtype)
        place = out.at[:, pl.ds(first * HEAD_SIZE, wide)]
        copies.append(pltpu.make_async_copy(total_ref.at[half], place, sems.at[i]))
        copies[-1].start()
    for copy in copies:
        copy.wait()


def finish(kept, home, first, width, buffers):
    whole = pl.BlockSpec(memory_space=pltpu.VMEM)
    anywhere = pl.BlockSpec(memory_space=pl.ANY)
    operands = in_vmem(kept, home)
    in_specs = [whole] * 2
    aliases = {}
    if buffers is not None:
        aliases = {2: 0, 3: 1}
        operands += buffers
        in_specs += [anywhere] * 2
    return pl.pallas_call(
        functools.partial(finish_kernel, first),
        in_specs=in_specs,
        out_specs=[anywhere] * 2,
        out_shape=[pltpu.HBM((kept.shape[0] // 2, width), kept.dtype)] * 2,
        scratch_shapes=[pltpu.VMEM(kept.shape, kept.dtype), pltpu.SemaphoreType.DMA((2,))],
        input_output_aliases=aliases,
        compiler_params=SMALL,
        cost_estimate=FREE,
        name="finish",
    )(*operands)


def shards(queries, keys, values, dout, doc_starts):
    rows, width = keys.shape
    kv_heads = width // HEAD_SIZE
    back = WINDOW_LENGTH // rows
    devices = lax.axis_size("seq") * lax.axis_size("head")
    if back != 2 or lax.axis_size("head") % 2 != 0:
        both = jnp.concatenate([keys, values], axis=0)
        halos = [shifted(both, j, devices) for j in range(1, back + 1)]
        dquery, own, *sent = attend(
            doc_starts, queries, dout, keys, values, [[halos[0]]], [[x] for x in halos[1:]], 0, 0,
            kv_heads, None, 1,
        )
        total = own.astype(jnp.float32)
        for j in range(back):
            total = total + shifted(sent[j], -(j + 1), devices).astype(jnp.float32)
        total = total.astype(jnp.bfloat16)
        return (dquery, total[:rows], total[rows:])

    starts = [sum(map(sum, GROUPS[:c])) for c in range(len(GROUPS))]
    packed = [pack(keys, values, start, sum(group), 1)[0] for start, group in zip(starts, GROUPS)]
    far = [shifted(x, 2, devices) for x in packed]
    early = [to_odd(after(x, *packed), devices) for x in packed]
    far[0] = after(far[0], *early)

    def work(start, first, heads, received, own_near, near, dquery):
        if near is None:
            near = to_even(received, devices)
        dquery, own, to_near, to_far = attend(
            doc_starts, queries, dout, keys, values, [[near], [own_near]], [[received]],
            start, first, heads, dquery, 1,
        )
        returned = swapped(to_near, devices)
        return near, dquery, *merge(to_far, own, returned)

    always = (doc_starts[0] | 1) != 0
    dquery, sums = None, []
    for start, group, received, own_near in zip(starts, GROUPS, far, early):
        near, first = None, start
        for heads in group:
            def skip(received, own_near, near, dquery):
                part = jnp.zeros((2 * rows, heads * HEAD_SIZE), received.dtype)
                near = jnp.zeros_like(received) if near is None else near
                return near, jnp.zeros_like(queries) if dquery is None else dquery, part, part

            near, dquery, send, kept = lax.cond(
                always,
                functools.partial(work, start, first, heads),
                skip,
                received,
                own_near,
                near,
                dquery,
            )
            sums.append((first, kept, shifted(send, -2, devices)))
            first += heads
    grads = None
    for first, kept, home in sums:
        grads = finish(kept, home, first, width, grads)
    dkey, dvalue = grads
    return (dquery, dkey, dvalue)


def solution(mesh):
    spec = P(AXES, None)
    return jax.shard_map(
        shards,
        mesh=mesh,
        in_specs=(spec, spec, spec, spec, P()),
        out_specs=(spec, spec, spec),
        check_vma=False,
    )
```

```python
import functools
import math

import jax
import jax.numpy as jnp
from jax import lax
from jax.experimental import pallas as pl
from jax.experimental.pallas import tpu as pltpu
from jax.sharding import PartitionSpec as P

HEAD_SIZE = 128
WINDOW_LENGTH = 512
AXES = ("seq", "head")
GROUPS = ((6,), (6,), (4,))
STEP = 2
UNIT = 128
STRIP = 32
VMEM_LIMIT = 16 * 1024 * 1024


scale_factor = 168.0 ** (-0.5)
log2_scale = scale_factor * math.log2(math.e)
negative = -1e30


def device_index():
    return lax.axis_index("seq") * lax.axis_size("head") + lax.axis_index("head")


def shifted(x, by, devices):
    pairs = [(i, i + by) for i in range(devices) if 0 <= i + by < devices]
    return lax.ppermute(x, AXES, pairs)


def swapped(x, devices):
    return lax.ppermute(x, AXES, [(i, i ^ 1) for i in range(devices)])


def to_odd(x, devices):
    return lax.ppermute(x, AXES, [(i, i + 1) for i in range(0, devices, 2)])


def to_even(x, devices):
    return lax.ppermute(x, AXES, [(i + 1, i) for i in range(0, devices, 2)])


def after(x, *others):
    return lax.optimization_barrier((x, *others))[0]


def dot_rows(left, right):
    return lax.dot_general(
        left, right, (((1,), (1,)), ((), ())), preferred_element_type=jnp.float32
    )


def dot_cols(left, right):
    return lax.dot_general(
        left, right, (((0,), (0,)), ((), ())), preferred_element_type=jnp.float32
    )


def dot(left, right):
    return jnp.dot(left, right, preferred_element_type=jnp.float32)


def merged(x, unit, pick_ref, at):
    if at >= unit:
        return x[at : at + STRIP]
    last = x.shape[0] - unit + at
    own = pick_ref[at : at + STRIP] > 0.5
    return jnp.where(own, x[last : last + STRIP], x[at : at + STRIP])


def spread(strips, unit, tri):
    edge = jnp.concatenate(strips[: unit // STRIP], axis=0)
    own = edge * tri
    return jnp.concatenate([edge - own] + strips[unit // STRIP :] + [own], axis=0)


def weigh(scores, dprobs, unit, bounds, pick_ref, tri):
    strips = range(0, scores.shape[0] - unit, STRIP)
    kept, peak = [], None
    for at in strips:
        s = jnp.minimum(merged(scores, unit, pick_ref, at), bounds[at : at + STRIP])
        kept.append(s)
        peak = s if peak is None else jnp.maximum(peak, s)
    peak = jnp.max(peak, axis=0, keepdims=True)
    low, dps = [], []
    total, weighted = 0.0, 0.0
    for at, s in zip(strips, kept):
        e = jnp.exp2((s - peak) * log2_scale)
        dp = merged(dprobs, unit, pick_ref, at)
        total = total + e
        weighted = weighted + e * dp
        low.append(e.astype(jnp.bfloat16))
        dps.append(dp)
    inverse = 1.0 / jnp.sum(total, axis=0, keepdims=True)
    delta = jnp.sum(weighted, axis=0, keepdims=True) * inverse
    ds = [e * (dp - delta).astype(jnp.bfloat16) for e, dp in zip(low, dps)]
    return spread(low, unit, tri), spread(ds, unit, tri), inverse


def products(q, g, k, low, ds, inverse):
    by_row = jnp.transpose(jnp.broadcast_to(inverse, (HEAD_SIZE, q.shape[0])))
    g_scaled = (g.astype(jnp.float32) * by_row).astype(jnp.bfloat16)
    q_scaled = (q.astype(jnp.float32) * (by_row * scale_factor)).astype(jnp.bfloat16)
    dv = dot(low, g_scaled)
    dk = dot(ds, q_scaled)
    dq = jnp.transpose(dot_cols(k, ds) * (inverse * scale_factor)).astype(jnp.bfloat16)
    return dq, dk, dv


def kernel(rows, back, group, split, pieces, starts_ref, q_ref, g_ref, k_ref, v_ref, *refs):
    pairs = [refs[2 * j : 2 * j + 2] for j in range(back + split)]
    outs = refs[len(refs) - (back + 1 + pieces) - 3 : len(refs) - 3]
    bound_ref, pick_ref, tri_ref = refs[-3:]
    dq_ref, own_ref, near_refs, far_refs = outs[0], outs[1], outs[2 : 2 + pieces], outs[2 + pieces :]
    unit = min(UNIT, rows)
    units = rows // unit
    columns = group * unit
    span = back * rows

    @pl.when(pl.program_id(0) == 0)
    def _():
        col = lax.broadcasted_iota(jnp.int32, (unit, columns), 1) % unit
        row = lax.broadcasted_iota(jnp.int32, (unit, columns), 0)
        own = row <= col
        pick_ref[...] = own.astype(jnp.float32)
        tri_ref[...] = pick_ref[...].astype(jnp.bfloat16)
        for u in range(units):
            base = device_index() * rows + u * unit
            pos = base + col[:1]
            start = jnp.zeros_like(pos)
            for doc in range(starts_ref.shape[0]):
                at = starts_ref[doc]
                start = jnp.where(pos >= at, at, start)
            start = jnp.broadcast_to(start, (unit, columns))
            for at in range(0, span, unit):
                key_pos = base - span + at + row
                if at == 0:
                    key_pos = jnp.where(own, key_pos + span, key_pos)
                bound_ref[u, at : at + unit] = jnp.where(key_pos >= start, jnp.inf, negative)

    tri = tri_ref[...]
    heads = range(k_ref.shape[1] // HEAD_SIZE)
    works = []
    for h in heads:
        at = slice(h * HEAD_SIZE, (h + 1) * HEAD_SIZE)

        def gathered(own, half):
            blocks = [pair[half][:, at] for pair in pairs]
            if split:
                blocks[:2] = [blocks[0] + blocks[1]]
            return jnp.concatenate(blocks[::-1] + [own[:, at]], axis=0)

        k_all = gathered(k_ref, 0)
        v_all = gathered(v_ref, 1)
        for u in range(units):
            of_rows = slice(u * unit, (u + 1) * unit)
            wide = [
                slice((h * group + m) * HEAD_SIZE, (h * group + m + 1) * HEAD_SIZE)
                for m in range(group)
            ]
            q = jnp.concatenate([q_ref[of_rows, w] for w in wide], axis=0)
            g = jnp.concatenate([g_ref[of_rows, w] for w in wide], axis=0)
            seen = slice(u * unit, u * unit + span + unit)
            works.append((h, u, of_rows, wide, q, g, k_all[seen], v_all[seen]))

    def begin(work):
        h, u, of_rows, wide, q, g, k, v = work
        return dot_rows(k, q), dot_rows(v, g)

    sums = {}
    ahead = begin(works[0])
    for i, work in enumerate(works):
        h, u, of_rows, wide, q, g, k, v = work
        scores, dprobs = ahead
        if i + 1 < len(works):
            ahead = begin(works[i + 1])
        low, ds, inverse = weigh(scores, dprobs, unit, bound_ref.at[u], pick_ref, tri)
        dq, dk, dv = products(q, g, k, low, ds, inverse)
        for m, w in enumerate(wide):
            dq_ref[of_rows, w] = dq[m * unit : (m + 1) * unit]
        for name, term in (("k", dk), ("v", dv)):
            for j in range((span + unit) // unit):
                key = (name, u + j)
                piece = term[j * unit : (j + 1) * unit]
                sums[key] = piece if key not in sums else sums[key] + piece
        if u + 1 < units:
            continue
        at = slice(h * HEAD_SIZE, (h + 1) * HEAD_SIZE)
        order = [[x] for x in far_refs[::-1]] + [near_refs, [own_ref]]
        for j, arrays in enumerate(order):
            height = 2 * rows // len(arrays)
            for name, below in (("k", 0), ("v", rows)):
                for of_unit in range(units):
                    piece, to = divmod(below + of_unit * unit, height)
                    total = sums[(name, j * units + of_unit)].astype(jnp.bfloat16)
                    arrays[piece][to : to + unit, at] = total
        sums = {}


def attend(
    doc_starts, queries, dout, keys, values, near, others, start, first, heads, buffer, pieces
):
    rows, width = keys.shape
    back = 1 + len(others)
    group = queries.shape[1] // width
    step = STEP * HEAD_SIZE
    unit = min(UNIT, rows)

    def part(height, wide, offset, row=0):
        return pl.BlockSpec((height, wide), lambda i: (row, offset // STEP + i))

    wide = part(rows, group * step, first)
    narrow = part(rows, step, first)
    smem = pl.BlockSpec(memory_space=pltpu.SMEM)
    operands = [doc_starts, queries, dout, keys, values]
    in_specs = [smem, wide, wide, narrow, narrow]
    for pair in near + others:
        operands += [pair[0], pair[-1]]
        in_specs += [part(rows, step, first - start, row) for row in (0, 2 - len(pair))]
    if len(near) == 2:
        operands[5:] = [pltpu.with_memory_space_constraint(x, pltpu.VMEM) for x in operands[5:]]
    aliases = {}
    if buffer is not None:
        aliases = {len(operands): 0}
        operands.append(buffer)
        in_specs.append(pl.BlockSpec(memory_space=pl.ANY))
    whole = (2 * rows, heads * HEAD_SIZE)
    outs = [whole] + [(2 * rows // pieces, heads * HEAD_SIZE)] * pieces + [whole] * (back - 1)
    outs = [queries.shape] + outs
    return pl.pallas_call(
        functools.partial(kernel, rows, back, group, len(near) == 2, pieces),
        grid=(heads // STEP,),
        in_specs=in_specs,
        out_specs=[wide] + [part(shape[0], step, 0) for shape in outs[1:]],
        out_shape=[jax.ShapeDtypeStruct(outs[0], jnp.bfloat16)]
        + [pltpu.VMEM(shape, jnp.bfloat16) for shape in outs[1:]],
        scratch_shapes=[
            pltpu.VMEM((rows // unit, back * rows, group * unit), jnp.float32),
            pltpu.VMEM((unit, group * unit), jnp.float32),
            pltpu.VMEM((unit, group * unit), jnp.bfloat16),
        ],
        input_output_aliases=aliases,
        compiler_params=pltpu.CompilerParams(vmem_limit_bytes=VMEM_LIMIT),
        cost_estimate=pl.CostEstimate(flops=1, bytes_accessed=1, transcendentals=0),
        name="attend",
    )(*operands)


def pack_kernel(first, k_ref, v_ref, *refs):
    outs, sems = refs[:-1], refs[-1]
    rows, wide = k_ref.shape[0], outs[0].shape[1]
    columns = pl.ds(first * HEAD_SIZE, wide)
    copies = []
    for i, ref in enumerate((k_ref, v_ref)):
        place = outs[i] if len(outs) == 2 else outs[0].at[pl.ds(i * rows, rows)]
        copies.append(pltpu.make_async_copy(ref.at[:, columns], place, sems.at[i]))
        copies[-1].start()
    for copy in copies:
        copy.wait()


def pack(keys, values, first, heads, arrays):
    rows, wide = keys.shape[0], heads * HEAD_SIZE
    keys, values = (pltpu.with_memory_space_constraint(x, pltpu.HBM) for x in (keys, values))
    shape = (2 * rows // arrays, wide)
    return pl.pallas_call(
        functools.partial(pack_kernel, first),
        in_specs=[pl.BlockSpec(memory_space=pl.ANY)] * 2,
        out_specs=[pl.BlockSpec(memory_space=pltpu.VMEM)] * arrays,
        out_shape=[pltpu.VMEM(shape, keys.dtype)] * arrays,
        scratch_shapes=[pltpu.SemaphoreType.DMA((2,))],
        compiler_params=pltpu.CompilerParams(vmem_limit_bytes=4 * 1024 * 1024),
        name="pack",
    )(keys, values)


SMALL = pltpu.CompilerParams(vmem_limit_bytes=6 * 1024 * 1024)
FREE = pl.CostEstimate(flops=1, bytes_accessed=1, transcendentals=0)


def in_vmem(*arrays):
    return [pltpu.with_memory_space_constraint(x, pltpu.VMEM) for x in arrays]


def merge_kernel(far_ref, own_ref, back_ref, send_ref, kept_ref):
    odd = device_index() % 2 == 1

    @pl.when(odd)
    def _():
        total = far_ref[...].astype(jnp.float32) + back_ref[...].astype(jnp.float32)
        send_ref[...] = total.astype(send_ref.dtype)
        kept_ref[...] = own_ref[...]

    @pl.when(jnp.logical_not(odd))
    def _():
        send_ref[...] = far_ref[...]
        total = own_ref[...].astype(jnp.float32) + back_ref[...].astype(jnp.float32)
        kept_ref[...] = total.astype(kept_ref.dtype)


def merge(far, own, back):
    whole = pl.BlockSpec(memory_space=pltpu.VMEM)
    return pl.pallas_call(
        merge_kernel,
        in_specs=[whole] * 3,
        out_specs=[whole] * 2,
        out_shape=[pltpu.VMEM(far.shape, far.dtype)] * 2,
        compiler_params=SMALL,
        cost_estimate=FREE,
        name="merge",
    )(*in_vmem(far, own, back))


def finish_kernel(first, kept_ref, home_ref, *refs):
    outs, total_ref, sems = refs[-4:-2], refs[-2], refs[-1]
    rows, wide = kept_ref.shape[0] // 2, kept_ref.shape[1]
    copies = []
    for i, out in enumerate(outs):
        half = slice(i * rows, (i + 1) * rows)
        total = kept_ref[half].astype(jnp.float32) + home_ref[half].astype(jnp.float32)
        total_ref[half] = total.astype(total_ref.dtype)
        place = out.at[:, pl.ds(first * HEAD_SIZE, wide)]
        copies.append(pltpu.make_async_copy(total_ref.at[half], place, sems.at[i]))
        copies[-1].start()
    for copy in copies:
        copy.wait()


def finish(kept, home, first, width, buffers):
    whole = pl.BlockSpec(memory_space=pltpu.VMEM)
    anywhere = pl.BlockSpec(memory_space=pl.ANY)
    operands = in_vmem(kept, home)
    in_specs = [whole] * 2
    aliases = {}
    if buffers is not None:
        aliases = {2: 0, 3: 1}
        operands += buffers
        in_specs += [anywhere] * 2
    return pl.pallas_call(
        functools.partial(finish_kernel, first),
        in_specs=in_specs,
        out_specs=[anywhere] * 2,
        out_shape=[pltpu.HBM((kept.shape[0] // 2, width), kept.dtype)] * 2,
        scratch_shapes=[pltpu.VMEM(kept.shape, kept.dtype), pltpu.SemaphoreType.DMA((2,))],
        input_output_aliases=aliases,
        compiler_params=SMALL,
        cost_estimate=FREE,
        name="finish",
    )(*operands)


def shards(queries, keys, values, dout, doc_starts):
    rows, width = keys.shape
    kv_heads = width // HEAD_SIZE
    back = WINDOW_LENGTH // rows
    devices = lax.axis_size("seq") * lax.axis_size("head")
    if back != 2 or lax.axis_size("head") % 2 != 0:
        both = jnp.concatenate([keys, values], axis=0)
        halos = [shifted(both, j, devices) for j in range(1, back + 1)]
        dquery, own, *sent = attend(
            doc_starts, queries, dout, keys, values, [[halos[0]]], [[x] for x in halos[1:]], 0, 0,
            kv_heads, None, 1,
        )
        total = own.astype(jnp.float32)
        for j in range(back):
            total = total + shifted(sent[j], -(j + 1), devices).astype(jnp.float32)
        total = total.astype(jnp.bfloat16)
        return (dquery, total[:rows], total[rows:])

    starts = [sum(map(sum, GROUPS[:c])) for c in range(len(GROUPS))]
    packed = [pack(keys, values, start, sum(group), 1)[0] for start, group in zip(starts, GROUPS)]
    far = [shifted(x, 2, devices) for x in packed]
    early = [to_odd(x, devices) for x in packed]
    far[0] = after(far[0], early[-1])

    def work(start, first, heads, received, own_near, near, dquery):
        if near is None:
            near = to_even(received, devices)
        dquery, own, to_near, to_far = attend(
            doc_starts, queries, dout, keys, values, [[near], [own_near]], [[received]],
            start, first, heads, dquery, 1,
        )
        returned = swapped(to_near, devices)
        return near, dquery, *merge(to_far, own, returned)

    always = (doc_starts[0] | 1) != 0
    dquery, sums = None, []
    for start, group, received, own_near in zip(starts, GROUPS, far, early):
        near, first = None, start
        for heads in group:
            def skip(received, own_near, near, dquery):
                part = jnp.zeros((2 * rows, heads * HEAD_SIZE), received.dtype)
                near = jnp.zeros_like(received) if near is None else near
                return near, jnp.zeros_like(queries) if dquery is None else dquery, part, part

            near, dquery, send, kept = lax.cond(
                always,
                functools.partial(work, start, first, heads),
                skip,
                received,
                own_near,
                near,
                dquery,
            )
            if len(sums) == 1:
                send = after(send, *far)
            sums.append((first, kept, shifted(send, -2, devices)))
            first += heads
    grads = None
    for first, kept, home in sums:
        grads = finish(kept, home, first, width, grads)
    dkey, dvalue = grads
    return (dquery, dkey, dvalue)


def solution(mesh):
    spec = P(AXES, None)
    return jax.shard_map(
        shards,
        mesh=mesh,
        in_specs=(spec, spec, spec, spec, P()),
        out_specs=(spec, spec, spec),
        check_vma=False,
    )
```

```python
import functools
import math

import jax
import jax.numpy as jnp
from jax import lax
from jax.experimental import pallas as pl
from jax.experimental.pallas import tpu as pltpu
from jax.sharding import PartitionSpec as P

HEAD_SIZE = 128
WINDOW_LENGTH = 512
AXES = ("seq", "head")
GROUPS = ((6,), (6,), (4,))
STEP = 2
UNIT = 128
STRIP = 32
VMEM_LIMIT = 16 * 1024 * 1024


scale_factor = 168.0 ** (-0.5)
log2_scale = scale_factor * math.log2(math.e)
negative = -1e30


def device_index():
    return lax.axis_index("seq") * lax.axis_size("head") + lax.axis_index("head")


def shifted(x, by, devices):
    pairs = [(i, i + by) for i in range(devices) if 0 <= i + by < devices]
    return lax.ppermute(x, AXES, pairs)


def swapped(x, devices):
    return lax.ppermute(x, AXES, [(i, i ^ 1) for i in range(devices)])


def to_odd(x, devices):
    return lax.ppermute(x, AXES, [(i, i + 1) for i in range(0, devices, 2)])


def to_even(x, devices):
    return lax.ppermute(x, AXES, [(i + 1, i) for i in range(0, devices, 2)])


def after(x, *others):
    return lax.optimization_barrier((x, *others))[0]


def dot_rows(left, right):
    return lax.dot_general(
        left, right, (((1,), (1,)), ((), ())), preferred_element_type=jnp.float32
    )


def dot_cols(left, right):
    return lax.dot_general(
        left, right, (((0,), (0,)), ((), ())), preferred_element_type=jnp.float32
    )


def dot(left, right):
    return jnp.dot(left, right, preferred_element_type=jnp.float32)


def merged(x, unit, pick_ref, at):
    if at >= unit:
        return x[at : at + STRIP]
    last = x.shape[0] - unit + at
    own = pick_ref[at : at + STRIP] > 0.5
    return jnp.where(own, x[last : last + STRIP], x[at : at + STRIP])


def spread(strips, unit, tri):
    edge = jnp.concatenate(strips[: unit // STRIP], axis=0)
    own = edge * tri
    return jnp.concatenate([edge - own] + strips[unit // STRIP :] + [own], axis=0)


def weigh(scores, dprobs, unit, bounds, pick_ref, tri):
    strips = range(0, scores.shape[0] - unit, STRIP)
    kept, peak = [], None
    for at in strips:
        s = jnp.minimum(merged(scores, unit, pick_ref, at), bounds[at : at + STRIP])
        kept.append(s)
        peak = s if peak is None else jnp.maximum(peak, s)
    peak = jnp.max(peak, axis=0, keepdims=True)
    low, dps = [], []
    total, weighted = 0.0, 0.0
    for at, s in zip(strips, kept):
        e = jnp.exp2((s - peak) * log2_scale)
        dp = merged(dprobs, unit, pick_ref, at)
        total = total + e
        weighted = weighted + e * dp
        low.append(e.astype(jnp.bfloat16))
        dps.append(dp)
    inverse = 1.0 / jnp.sum(total, axis=0, keepdims=True)
    delta = jnp.sum(weighted, axis=0, keepdims=True) * inverse
    ds = [e * (dp - delta).astype(jnp.bfloat16) for e, dp in zip(low, dps)]
    return spread(low, unit, tri), spread(ds, unit, tri), inverse


def products(q, g, k, low, ds, inverse):
    by_row = jnp.transpose(jnp.broadcast_to(inverse, (HEAD_SIZE, q.shape[0])))
    g_scaled = (g.astype(jnp.float32) * by_row).astype(jnp.bfloat16)
    q_scaled = (q.astype(jnp.float32) * (by_row * scale_factor)).astype(jnp.bfloat16)
    dv = dot(low, g_scaled)
    dk = dot(ds, q_scaled)
    dq = jnp.transpose(dot_cols(k, ds) * (inverse * scale_factor)).astype(jnp.bfloat16)
    return dq, dk, dv


def kernel(rows, back, group, split, pieces, starts_ref, q_ref, g_ref, k_ref, v_ref, *refs):
    pairs = [refs[2 * j : 2 * j + 2] for j in range(back + split)]
    outs = refs[len(refs) - (back + 1 + pieces) - 3 : len(refs) - 3]
    bound_ref, pick_ref, tri_ref = refs[-3:]
    dq_ref, own_ref, near_refs, far_refs = outs[0], outs[1], outs[2 : 2 + pieces], outs[2 + pieces :]
    unit = min(UNIT, rows)
    units = rows // unit
    columns = group * unit
    span = back * rows

    @pl.when(pl.program_id(0) == 0)
    def _():
        col = lax.broadcasted_iota(jnp.int32, (unit, columns), 1) % unit
        row = lax.broadcasted_iota(jnp.int32, (unit, columns), 0)
        own = row <= col
        pick_ref[...] = own.astype(jnp.float32)
        tri_ref[...] = pick_ref[...].astype(jnp.bfloat16)
        for u in range(units):
            base = device_index() * rows + u * unit
            pos = base + col[:1]
            start = jnp.zeros_like(pos)
            for doc in range(starts_ref.shape[0]):
                at = starts_ref[doc]
                start = jnp.where(pos >= at, at, start)
            start = jnp.broadcast_to(start, (unit, columns))
            for at in range(0, span, unit):
                key_pos = base - span + at + row
                if at == 0:
                    key_pos = jnp.where(own, key_pos + span, key_pos)
                bound_ref[u, at : at + unit] = jnp.where(key_pos >= start, jnp.inf, negative)

    tri = tri_ref[...]
    heads = range(k_ref.shape[1] // HEAD_SIZE)
    works = []
    for h in heads:
        at = slice(h * HEAD_SIZE, (h + 1) * HEAD_SIZE)

        def gathered(own, half):
            blocks = [pair[half][:, at] for pair in pairs]
            if split:
                blocks[:2] = [blocks[0] + blocks[1]]
            return jnp.concatenate(blocks[::-1] + [own[:, at]], axis=0)

        k_all = gathered(k_ref, 0)
        v_all = gathered(v_ref, 1)
        for u in range(units):
            of_rows = slice(u * unit, (u + 1) * unit)
            wide = [
                slice((h * group + m) * HEAD_SIZE, (h * group + m + 1) * HEAD_SIZE)
                for m in range(group)
            ]
            q = jnp.concatenate([q_ref[of_rows, w] for w in wide], axis=0)
            g = jnp.concatenate([g_ref[of_rows, w] for w in wide], axis=0)
            seen = slice(u * unit, u * unit + span + unit)
            works.append((h, u, of_rows, wide, q, g, k_all[seen], v_all[seen]))

    def begin(work):
        h, u, of_rows, wide, q, g, k, v = work
        return dot_rows(k, q), dot_rows(v, g)

    sums = {}
    ahead = begin(works[0])
    for i, work in enumerate(works):
        h, u, of_rows, wide, q, g, k, v = work
        scores, dprobs = ahead
        if i + 1 < len(works):
            ahead = begin(works[i + 1])
        low, ds, inverse = weigh(scores, dprobs, unit, bound_ref.at[u], pick_ref, tri)
        dq, dk, dv = products(q, g, k, low, ds, inverse)
        for m, w in enumerate(wide):
            dq_ref[of_rows, w] = dq[m * unit : (m + 1) * unit]
        for name, term in (("k", dk), ("v", dv)):
            for j in range((span + unit) // unit):
                key = (name, u + j)
                piece = term[j * unit : (j + 1) * unit]
                sums[key] = piece if key not in sums else sums[key] + piece
        if u + 1 < units:
            continue
        at = slice(h * HEAD_SIZE, (h + 1) * HEAD_SIZE)
        order = [[x] for x in far_refs[::-1]] + [near_refs, [own_ref]]
        for j, arrays in enumerate(order):
            height = 2 * rows // len(arrays)
            for name, below in (("k", 0), ("v", rows)):
                for of_unit in range(units):
                    piece, to = divmod(below + of_unit * unit, height)
                    total = sums[(name, j * units + of_unit)].astype(jnp.bfloat16)
                    arrays[piece][to : to + unit, at] = total
        sums = {}


def attend(
    doc_starts, queries, dout, keys, values, near, others, start, first, heads, buffer, pieces
):
    rows, width = keys.shape
    back = 1 + len(others)
    group = queries.shape[1] // width
    step = STEP * HEAD_SIZE
    unit = min(UNIT, rows)

    def part(height, wide, offset, row=0):
        return pl.BlockSpec((height, wide), lambda i: (row, offset // STEP + i))

    wide = part(rows, group * step, first)
    narrow = part(rows, step, first)
    smem = pl.BlockSpec(memory_space=pltpu.SMEM)
    operands = [doc_starts, queries, dout, keys, values]
    in_specs = [smem, wide, wide, narrow, narrow]
    for pair in near + others:
        operands += [pair[0], pair[-1]]
        in_specs += [part(rows, step, first - start, row) for row in (0, 2 - len(pair))]
    if len(near) == 2:
        operands[5:] = [pltpu.with_memory_space_constraint(x, pltpu.VMEM) for x in operands[5:]]
    aliases = {}
    if buffer is not None:
        aliases = {len(operands): 0}
        operands.append(buffer)
        in_specs.append(pl.BlockSpec(memory_space=pl.ANY))
    whole = (2 * rows, heads * HEAD_SIZE)
    outs = [whole] + [(2 * rows // pieces, heads * HEAD_SIZE)] * pieces + [whole] * (back - 1)
    outs = [queries.shape] + outs
    return pl.pallas_call(
        functools.partial(kernel, rows, back, group, len(near) == 2, pieces),
        grid=(heads // STEP,),
        in_specs=in_specs,
        out_specs=[wide] + [part(shape[0], step, 0) for shape in outs[1:]],
        out_shape=[jax.ShapeDtypeStruct(outs[0], jnp.bfloat16)]
        + [pltpu.VMEM(shape, jnp.bfloat16) for shape in outs[1:]],
        scratch_shapes=[
            pltpu.VMEM((rows // unit, back * rows, group * unit), jnp.float32),
            pltpu.VMEM((unit, group * unit), jnp.float32),
            pltpu.VMEM((unit, group * unit), jnp.bfloat16),
        ],
        input_output_aliases=aliases,
        compiler_params=pltpu.CompilerParams(vmem_limit_bytes=VMEM_LIMIT),
        cost_estimate=pl.CostEstimate(flops=1, bytes_accessed=1, transcendentals=0),
        name="attend",
    )(*operands)


def pack_kernel(first, k_ref, v_ref, *refs):
    outs, sems = refs[:-1], refs[-1]
    rows, wide = k_ref.shape[0], outs[0].shape[1]
    columns = pl.ds(first * HEAD_SIZE, wide)
    copies = []
    for i, ref in enumerate((k_ref, v_ref)):
        place = outs[i] if len(outs) == 2 else outs[0].at[pl.ds(i * rows, rows)]
        copies.append(pltpu.make_async_copy(ref.at[:, columns], place, sems.at[i]))
        copies[-1].start()
    for copy in copies:
        copy.wait()


def pack(keys, values, first, heads, arrays):
    rows, wide = keys.shape[0], heads * HEAD_SIZE
    keys, values = (pltpu.with_memory_space_constraint(x, pltpu.HBM) for x in (keys, values))
    shape = (2 * rows // arrays, wide)
    return pl.pallas_call(
        functools.partial(pack_kernel, first),
        in_specs=[pl.BlockSpec(memory_space=pl.ANY)] * 2,
        out_specs=[pl.BlockSpec(memory_space=pltpu.VMEM)] * arrays,
        out_shape=[pltpu.VMEM(shape, keys.dtype)] * arrays,
        scratch_shapes=[pltpu.SemaphoreType.DMA((2,))],
        compiler_params=pltpu.CompilerParams(vmem_limit_bytes=4 * 1024 * 1024),
        name="pack",
    )(keys, values)


SMALL = pltpu.CompilerParams(vmem_limit_bytes=6 * 1024 * 1024)
FREE = pl.CostEstimate(flops=1, bytes_accessed=1, transcendentals=0)


def in_vmem(*arrays):
    return [pltpu.with_memory_space_constraint(x, pltpu.VMEM) for x in arrays]


def merge_kernel(far_ref, own_ref, back_ref, send_ref, kept_ref):
    odd = device_index() % 2 == 1

    @pl.when(odd)
    def _():
        total = far_ref[...].astype(jnp.float32) + back_ref[...].astype(jnp.float32)
        send_ref[...] = total.astype(send_ref.dtype)
        kept_ref[...] = own_ref[...]

    @pl.when(jnp.logical_not(odd))
    def _():
        send_ref[...] = far_ref[...]
        total = own_ref[...].astype(jnp.float32) + back_ref[...].astype(jnp.float32)
        kept_ref[...] = total.astype(kept_ref.dtype)


def merge(far, own, back):
    whole = pl.BlockSpec(memory_space=pltpu.VMEM)
    return pl.pallas_call(
        merge_kernel,
        in_specs=[whole] * 3,
        out_specs=[whole] * 2,
        out_shape=[pltpu.VMEM(far.shape, far.dtype)] * 2,
        compiler_params=SMALL,
        cost_estimate=FREE,
        name="merge",
    )(*in_vmem(far, own, back))


def finish_kernel(first, kept_ref, home_ref, *refs):
    outs, total_ref, sems = refs[-4:-2], refs[-2], refs[-1]
    rows, wide = kept_ref.shape[0] // 2, kept_ref.shape[1]
    copies = []
    for i, out in enumerate(outs):
        half = slice(i * rows, (i + 1) * rows)
        total = kept_ref[half].astype(jnp.float32) + home_ref[half].astype(jnp.float32)
        total_ref[half] = total.astype(total_ref.dtype)
        place = out.at[:, pl.ds(first * HEAD_SIZE, wide)]
        copies.append(pltpu.make_async_copy(total_ref.at[half], place, sems.at[i]))
        copies[-1].start()
    for copy in copies:
        copy.wait()


def finish(kept, home, first, width, buffers):
    whole = pl.BlockSpec(memory_space=pltpu.VMEM)
    anywhere = pl.BlockSpec(memory_space=pl.ANY)
    operands = in_vmem(kept, home)
    in_specs = [whole] * 2
    aliases = {}
    if buffers is not None:
        aliases = {2: 0, 3: 1}
        operands += buffers
        in_specs += [anywhere] * 2
    return pl.pallas_call(
        functools.partial(finish_kernel, first),
        in_specs=in_specs,
        out_specs=[anywhere] * 2,
        out_shape=[pltpu.HBM((kept.shape[0] // 2, width), kept.dtype)] * 2,
        scratch_shapes=[pltpu.VMEM(kept.shape, kept.dtype), pltpu.SemaphoreType.DMA((2,))],
        input_output_aliases=aliases,
        compiler_params=SMALL,
        cost_estimate=pl.CostEstimate(flops=600000000, bytes_accessed=1, transcendentals=0),
        name="finish",
    )(*operands)


def shards(queries, keys, values, dout, doc_starts):
    rows, width = keys.shape
    kv_heads = width // HEAD_SIZE
    back = WINDOW_LENGTH // rows
    devices = lax.axis_size("seq") * lax.axis_size("head")
    if back != 2 or lax.axis_size("head") % 2 != 0:
        both = jnp.concatenate([keys, values], axis=0)
        halos = [shifted(both, j, devices) for j in range(1, back + 1)]
        dquery, own, *sent = attend(
            doc_starts, queries, dout, keys, values, [[halos[0]]], [[x] for x in halos[1:]], 0, 0,
            kv_heads, None, 1,
        )
        total = own.astype(jnp.float32)
        for j in range(back):
            total = total + shifted(sent[j], -(j + 1), devices).astype(jnp.float32)
        total = total.astype(jnp.bfloat16)
        return (dquery, total[:rows], total[rows:])

    starts = [sum(map(sum, GROUPS[:c])) for c in range(len(GROUPS))]
    packed = [pack(keys, values, start, sum(group), 1)[0] for start, group in zip(starts, GROUPS)]
    far = [shifted(x, 2, devices) for x in packed]
    early = [to_odd(x, devices) for x in packed]

    def work(start, first, heads, received, own_near, near, dquery):
        if near is None:
            near = to_even(received, devices)
        dquery, own, to_near, to_far = attend(
            doc_starts, queries, dout, keys, values, [[near], [own_near]], [[received]],
            start, first, heads, dquery, 1,
        )
        returned = swapped(to_near, devices)
        return near, dquery, *merge(to_far, own, returned)

    always = (doc_starts[0] | 1) != 0
    dquery, sums = None, []
    for start, group, received, own_near in zip(starts, GROUPS, far, early):
        near, first = None, start
        for heads in group:
            def skip(received, own_near, near, dquery):
                part = jnp.zeros((2 * rows, heads * HEAD_SIZE), received.dtype)
                near = jnp.zeros_like(received) if near is None else near
                return near, jnp.zeros_like(queries) if dquery is None else dquery, part, part

            near, dquery, send, kept = lax.cond(
                always,
                functools.partial(work, start, first, heads),
                skip,
                received,
                own_near,
                near,
                dquery,
            )
            if len(sums) == 1:
                send = after(send, *far)
            sums.append((first, kept, shifted(send, -2, devices)))
            first += heads
    grads = None
    for first, kept, home in sums:
        grads = finish(kept, home, first, width, grads)
    dkey, dvalue = grads
    return (dquery, dkey, dvalue)


def solution(mesh):
    spec = P(AXES, None)
    return jax.shard_map(
        shards,
        mesh=mesh,
        in_specs=(spec, spec, spec, spec, P()),
        out_specs=(spec, spec, spec),
        check_vma=False,
    )
```

```python
import functools
import math

import jax
import jax.numpy as jnp
from jax import lax
from jax.experimental import pallas as pl
from jax.experimental.pallas import tpu as pltpu
from jax.sharding import PartitionSpec as P

HEAD_SIZE = 128
WINDOW_LENGTH = 512
AXES = ("seq", "head")
GROUPS = ((6,), (8,), (2,))
STEP = 2
PIECES = 4
UNIT = 128
STRIP = 32
VMEM_LIMIT = 16 * 1024 * 1024


scale_factor = 168.0 ** (-0.5)
log2_scale = scale_factor * math.log2(math.e)
negative = -1e30


def device_index():
    return lax.axis_index("seq") * lax.axis_size("head") + lax.axis_index("head")


def shifted(x, by, devices):
    pairs = [(i, i + by) for i in range(devices) if 0 <= i + by < devices]
    return lax.ppermute(x, AXES, pairs)


def swapped(x, devices):
    return lax.ppermute(x, AXES, [(i, i ^ 1) for i in range(devices)])


def to_odd(x, devices):
    return lax.ppermute(x, AXES, [(i, i + 1) for i in range(0, devices, 2)])


def to_even(x, devices):
    return lax.ppermute(x, AXES, [(i + 1, i) for i in range(0, devices, 2)])


def after(x, *others):
    return lax.optimization_barrier((x, *others))[0]


def dot_rows(left, right):
    return lax.dot_general(
        left, right, (((1,), (1,)), ((), ())), preferred_element_type=jnp.float32
    )


def dot_cols(left, right):
    return lax.dot_general(
        left, right, (((0,), (0,)), ((), ())), preferred_element_type=jnp.float32
    )


def dot(left, right):
    return jnp.dot(left, right, preferred_element_type=jnp.float32)


def merged(x, unit, pick_ref, at):
    if at >= unit:
        return x[at : at + STRIP]
    last = x.shape[0] - unit + at
    own = pick_ref[at : at + STRIP] > 0.5
    return jnp.where(own, x[last : last + STRIP], x[at : at + STRIP])


def spread(strips, unit, tri):
    edge = jnp.concatenate(strips[: unit // STRIP], axis=0)
    own = edge * tri
    return jnp.concatenate([edge - own] + strips[unit // STRIP :] + [own], axis=0)


def weigh(scores, dprobs, unit, bounds, pick_ref, tri):
    strips = range(0, scores.shape[0] - unit, STRIP)
    kept, peak = [], None
    for at in strips:
        s = jnp.minimum(merged(scores, unit, pick_ref, at), bounds[at : at + STRIP])
        kept.append(s)
        peak = s if peak is None else jnp.maximum(peak, s)
    peak = jnp.max(peak, axis=0, keepdims=True)
    low, dps = [], []
    total, weighted = 0.0, 0.0
    for at, s in zip(strips, kept):
        e = jnp.exp2((s - peak) * log2_scale)
        dp = merged(dprobs, unit, pick_ref, at)
        total = total + e
        weighted = weighted + e * dp
        low.append(e.astype(jnp.bfloat16))
        dps.append(dp)
    inverse = 1.0 / jnp.sum(total, axis=0, keepdims=True)
    delta = jnp.sum(weighted, axis=0, keepdims=True) * inverse
    ds = [e * (dp - delta).astype(jnp.bfloat16) for e, dp in zip(low, dps)]
    return spread(low, unit, tri), spread(ds, unit, tri), inverse


def products(q, g, k, low, ds, inverse):
    by_row = jnp.transpose(jnp.broadcast_to(inverse, (HEAD_SIZE, q.shape[0])))
    g_scaled = (g.astype(jnp.float32) * by_row).astype(jnp.bfloat16)
    q_scaled = (q.astype(jnp.float32) * (by_row * scale_factor)).astype(jnp.bfloat16)
    dv = dot(low, g_scaled)
    dk = dot(ds, q_scaled)
    dq = jnp.transpose(dot_cols(k, ds) * (inverse * scale_factor)).astype(jnp.bfloat16)
    return dq, dk, dv


def kernel(rows, back, group, split, pieces, starts_ref, q_ref, g_ref, k_ref, v_ref, *refs):
    pairs = [refs[2 * j : 2 * j + 2] for j in range(back + split)]
    outs = refs[len(refs) - (back + 1 + pieces) - 3 : len(refs) - 3]
    bound_ref, pick_ref, tri_ref = refs[-3:]
    dq_ref, own_ref, near_refs, far_refs = outs[0], outs[1], outs[2 : 2 + pieces], outs[2 + pieces :]
    unit = min(UNIT, rows)
    units = rows // unit
    columns = group * unit
    span = back * rows

    @pl.when(pl.program_id(0) == 0)
    def _():
        col = lax.broadcasted_iota(jnp.int32, (unit, columns), 1) % unit
        row = lax.broadcasted_iota(jnp.int32, (unit, columns), 0)
        own = row <= col
        pick_ref[...] = own.astype(jnp.float32)
        tri_ref[...] = pick_ref[...].astype(jnp.bfloat16)
        for u in range(units):
            base = device_index() * rows + u * unit
            pos = base + col[:1]
            start = jnp.zeros_like(pos)
            for doc in range(starts_ref.shape[0]):
                at = starts_ref[doc]
                start = jnp.where(pos >= at, at, start)
            start = jnp.broadcast_to(start, (unit, columns))
            for at in range(0, span, unit):
                key_pos = base - span + at + row
                if at == 0:
                    key_pos = jnp.where(own, key_pos + span, key_pos)
                bound_ref[u, at : at + unit] = jnp.where(key_pos >= start, jnp.inf, negative)

    tri = tri_ref[...]
    heads = range(k_ref.shape[1] // HEAD_SIZE)
    works = []
    for h in heads:
        at = slice(h * HEAD_SIZE, (h + 1) * HEAD_SIZE)

        def gathered(own, half):
            blocks = [pair[half][:, at] for pair in pairs]
            if split:
                blocks[:2] = [blocks[0] + blocks[1]]
            return jnp.concatenate(blocks[::-1] + [own[:, at]], axis=0)

        k_all = gathered(k_ref, 0)
        v_all = gathered(v_ref, 1)
        for u in range(units):
            of_rows = slice(u * unit, (u + 1) * unit)
            wide = [
                slice((h * group + m) * HEAD_SIZE, (h * group + m + 1) * HEAD_SIZE)
                for m in range(group)
            ]
            q = jnp.concatenate([q_ref[of_rows, w] for w in wide], axis=0)
            g = jnp.concatenate([g_ref[of_rows, w] for w in wide], axis=0)
            seen = slice(u * unit, u * unit + span + unit)
            works.append((h, u, of_rows, wide, q, g, k_all[seen], v_all[seen]))

    def begin(work):
        h, u, of_rows, wide, q, g, k, v = work
        return dot_rows(k, q), dot_rows(v, g)

    sums = {}
    ahead = begin(works[0])
    for i, work in enumerate(works):
        h, u, of_rows, wide, q, g, k, v = work
        scores, dprobs = ahead
        if i + 1 < len(works):
            ahead = begin(works[i + 1])
        low, ds, inverse = weigh(scores, dprobs, unit, bound_ref.at[u], pick_ref, tri)
        dq, dk, dv = products(q, g, k, low, ds, inverse)
        for m, w in enumerate(wide):
            dq_ref[of_rows, w] = dq[m * unit : (m + 1) * unit]
        for name, term in (("k", dk), ("v", dv)):
            for j in range((span + unit) // unit):
                key = (name, u + j)
                piece = term[j * unit : (j + 1) * unit]
                sums[key] = piece if key not in sums else sums[key] + piece
        if u + 1 < units:
            continue
        at = slice(h * HEAD_SIZE, (h + 1) * HEAD_SIZE)
        order = [[x] for x in far_refs[::-1]] + [near_refs, [own_ref]]
        for j, arrays in enumerate(order):
            height = 2 * rows // len(arrays)
            for name, below in (("k", 0), ("v", rows)):
                for of_unit in range(units):
                    piece, to = divmod(below + of_unit * unit, height)
                    total = sums[(name, j * units + of_unit)].astype(jnp.bfloat16)
                    arrays[piece][to : to + unit, at] = total
        sums = {}


def attend(
    doc_starts, queries, dout, keys, values, near, others, start, first, heads, buffer, pieces
):
    rows, width = keys.shape
    back = 1 + len(others)
    group = queries.shape[1] // width
    step = STEP * HEAD_SIZE
    unit = min(UNIT, rows)

    def part(height, wide, offset, row=0):
        return pl.BlockSpec((height, wide), lambda i: (row, offset // STEP + i))

    wide = part(rows, group * step, first)
    narrow = part(rows, step, first)
    smem = pl.BlockSpec(memory_space=pltpu.SMEM)
    operands = [doc_starts, queries, dout, keys, values]
    in_specs = [smem, wide, wide, narrow, narrow]
    for pair in near + others:
        operands += [pair[0], pair[-1]]
        in_specs += [part(rows, step, first - start, row) for row in (0, 2 - len(pair))]
    if len(near) == 2:
        operands[5:] = [pltpu.with_memory_space_constraint(x, pltpu.VMEM) for x in operands[5:]]
    aliases = {}
    if buffer is not None:
        aliases = {len(operands): 0}
        operands.append(buffer)
        in_specs.append(pl.BlockSpec(memory_space=pl.ANY))
    whole = (2 * rows, heads * HEAD_SIZE)
    outs = [whole] + [(2 * rows // pieces, heads * HEAD_SIZE)] * pieces + [whole] * (back - 1)
    outs = [queries.shape] + outs
    return pl.pallas_call(
        functools.partial(kernel, rows, back, group, len(near) == 2, pieces),
        grid=(heads // STEP,),
        in_specs=in_specs,
        out_specs=[wide] + [part(shape[0], step, 0) for shape in outs[1:]],
        out_shape=[jax.ShapeDtypeStruct(outs[0], jnp.bfloat16)]
        + [pltpu.VMEM(shape, jnp.bfloat16) for shape in outs[1:]],
        scratch_shapes=[
            pltpu.VMEM((rows // unit, back * rows, group * unit), jnp.float32),
            pltpu.VMEM((unit, group * unit), jnp.float32),
            pltpu.VMEM((unit, group * unit), jnp.bfloat16),
        ],
        input_output_aliases=aliases,
        compiler_params=pltpu.CompilerParams(vmem_limit_bytes=VMEM_LIMIT),
        cost_estimate=pl.CostEstimate(flops=1, bytes_accessed=1, transcendentals=0),
        name="attend",
    )(*operands)


def pack_kernel(first, k_ref, v_ref, out_ref, sems):
    rows, wide = k_ref.shape[0], out_ref.shape[1]
    columns = pl.ds(first * HEAD_SIZE, wide)
    height = rows // PIECES
    copies = []
    for i in range(2 * PIECES):
        ref = (k_ref, v_ref)[i // PIECES]
        source = ref.at[pl.ds(i % PIECES * height, height), columns]
        copies.append(
            pltpu.make_async_copy(source, out_ref.at[pl.ds(i * height, height)], sems.at[i])
        )
        copies[-1].start()
    for copy in copies:
        copy.wait()


def pack(keys, values, first, heads):
    rows, wide = keys.shape[0], heads * HEAD_SIZE
    keys, values = (pltpu.with_memory_space_constraint(x, pltpu.HBM) for x in (keys, values))
    shape = (2 * rows, wide)
    return pl.pallas_call(
        functools.partial(pack_kernel, first),
        in_specs=[pl.BlockSpec(memory_space=pl.ANY)] * 2,
        out_specs=pl.BlockSpec(memory_space=pltpu.VMEM),
        out_shape=pltpu.VMEM(shape, keys.dtype),
        scratch_shapes=[pltpu.SemaphoreType.DMA((2 * PIECES,))],
        compiler_params=pltpu.CompilerParams(vmem_limit_bytes=4 * 1024 * 1024),
        name="pack",
    )(keys, values)


SMALL = pltpu.CompilerParams(vmem_limit_bytes=6 * 1024 * 1024)


def cost(flops):
    return pl.CostEstimate(flops=flops, bytes_accessed=1, transcendentals=0)


FREE = cost(1)


def step(x, flops):
    anywhere = pl.BlockSpec(memory_space=pl.ANY)
    return pl.pallas_call(
        lambda x_ref, out_ref: None,
        in_specs=[anywhere],
        out_specs=anywhere,
        out_shape=jax.ShapeDtypeStruct(x.shape, x.dtype),
        input_output_aliases={0: 0},
        compiler_params=SMALL,
        cost_estimate=cost(flops),
        name="step",
    )(x)


def in_vmem(*arrays):
    return [pltpu.with_memory_space_constraint(x, pltpu.VMEM) for x in arrays]


def merge_kernel(far_ref, own_ref, back_ref, send_ref, kept_ref):
    odd = device_index() % 2 == 1

    @pl.when(odd)
    def _():
        total = far_ref[...].astype(jnp.float32) + back_ref[...].astype(jnp.float32)
        send_ref[...] = total.astype(send_ref.dtype)
        kept_ref[...] = own_ref[...]

    @pl.when(jnp.logical_not(odd))
    def _():
        send_ref[...] = far_ref[...]
        total = own_ref[...].astype(jnp.float32) + back_ref[...].astype(jnp.float32)
        kept_ref[...] = total.astype(kept_ref.dtype)


def merge(far, own, back):
    whole = pl.BlockSpec(memory_space=pltpu.VMEM)
    return pl.pallas_call(
        merge_kernel,
        in_specs=[whole] * 3,
        out_specs=[whole] * 2,
        out_shape=[pltpu.VMEM(far.shape, far.dtype)] * 2,
        compiler_params=SMALL,
        cost_estimate=FREE,
        name="merge",
    )(*in_vmem(far, own, back))


def finish_kernel(first, kept_ref, home_ref, *refs):
    outs, total_ref, sems = refs[-4:-2], refs[-2], refs[-1]
    rows, wide = kept_ref.shape[0] // 2, kept_ref.shape[1]
    copies = []
    for i, out in enumerate(outs):
        half = slice(i * rows, (i + 1) * rows)
        total = kept_ref[half].astype(jnp.float32) + home_ref[half].astype(jnp.float32)
        total_ref[half] = total.astype(total_ref.dtype)
        place = out.at[:, pl.ds(first * HEAD_SIZE, wide)]
        copies.append(pltpu.make_async_copy(total_ref.at[half], place, sems.at[i]))
        copies[-1].start()
    for copy in copies:
        copy.wait()


def finish(kept, home, first, width, buffers):
    whole = pl.BlockSpec(memory_space=pltpu.VMEM)
    anywhere = pl.BlockSpec(memory_space=pl.ANY)
    operands = in_vmem(kept, home)
    in_specs = [whole] * 2
    aliases = {}
    if buffers is not None:
        aliases = {2: 0, 3: 1}
        operands += buffers
        in_specs += [anywhere] * 2
    return pl.pallas_call(
        functools.partial(finish_kernel, first),
        in_specs=in_specs,
        out_specs=[anywhere] * 2,
        out_shape=[pltpu.HBM((kept.shape[0] // 2, width), kept.dtype)] * 2,
        scratch_shapes=[pltpu.VMEM(kept.shape, kept.dtype), pltpu.SemaphoreType.DMA((2,))],
        input_output_aliases=aliases,
        compiler_params=SMALL,
        cost_estimate=cost(3000000000 if first == 0 else 1),
        name="finish",
    )(*operands)


def shards(queries, keys, values, dout, doc_starts):
    rows, width = keys.shape
    kv_heads = width // HEAD_SIZE
    back = WINDOW_LENGTH // rows
    devices = lax.axis_size("seq") * lax.axis_size("head")
    if back != 2 or lax.axis_size("head") % 2 != 0:
        both = jnp.concatenate([keys, values], axis=0)
        halos = [shifted(both, j, devices) for j in range(1, back + 1)]
        dquery, own, *sent = attend(
            doc_starts, queries, dout, keys, values, [[halos[0]]], [[x] for x in halos[1:]], 0, 0,
            kv_heads, None, 1,
        )
        total = own.astype(jnp.float32)
        for j in range(back):
            total = total + shifted(sent[j], -(j + 1), devices).astype(jnp.float32)
        total = total.astype(jnp.bfloat16)
        return (dquery, total[:rows], total[rows:])

    starts = [sum(map(sum, GROUPS[:c])) for c in range(len(GROUPS))]
    packed = [pack(keys, values, start, sum(group)) for start, group in zip(starts, GROUPS)]
    far = [shifted(x, 2, devices) for x in packed]
    early = [to_odd(x, devices) for x in packed]
    far[-1], early[-1] = lax.optimization_barrier((far[-1], early[-1]))
    far[0], far[-1] = step(far[0], 3000000000), step(far[-1], 6500000000)

    def work(start, first, heads, received, own_near, near, dquery):
        if near is None:
            near = to_even(received, devices)
        dquery, own, to_near, to_far = attend(
            doc_starts, queries, dout, keys, values, [[near], [own_near]], [[received]],
            start, first, heads, dquery, 1,
        )
        returned = swapped(to_near, devices)
        return near, dquery, *merge(to_far, own, returned)

    always = (doc_starts[0] | 1) != 0
    dquery, sums = None, []
    for start, group, received, own_near in zip(starts, GROUPS, far, early):
        near, first = None, start
        for heads in group:
            def skip(received, own_near, near, dquery):
                part = jnp.zeros((2 * rows, heads * HEAD_SIZE), received.dtype)
                near = jnp.zeros_like(received) if near is None else near
                return near, jnp.zeros_like(queries) if dquery is None else dquery, part, part

            near, dquery, send, kept = lax.cond(
                always,
                functools.partial(work, start, first, heads),
                skip,
                received,
                own_near,
                near,
                dquery,
            )
            sums.append((first, kept, shifted(send, -2, devices)))
            first += heads
    grads = None
    for first, kept, home in sums:
        grads = finish(kept, home, first, width, grads)
    dkey, dvalue = grads
    return (dquery, dkey, dvalue)


def solution(mesh):
    spec = P(AXES, None)
    return jax.shard_map(
        shards,
        mesh=mesh,
        in_specs=(spec, spec, spec, spec, P()),
        out_specs=(spec, spec, spec),
        check_vma=False,
    )
```

```python
import functools
import math

import jax
import jax.numpy as jnp
from jax import lax
from jax.experimental import pallas as pl
from jax.experimental.pallas import tpu as pltpu
from jax.sharding import PartitionSpec as P

HEAD_SIZE = 128
WINDOW_LENGTH = 512
AXES = ("seq", "head")
GROUPS = (6, 6, 4)
STEP = 2
UNIT = 128
STRIP = 32
VMEM_LIMIT = 16 * 1024 * 1024


scale_factor = 168.0 ** (-0.5)
log2_scale = scale_factor * math.log2(math.e)
negative = -1e30


def device_index():
    return lax.axis_index("seq") * lax.axis_size("head") + lax.axis_index("head")


def shifted(x, by, devices):
    pairs = [(i, i + by) for i in range(devices) if 0 <= i + by < devices]
    return lax.ppermute(x, AXES, pairs)


def swapped(x, devices):
    return lax.ppermute(x, AXES, [(i, i ^ 1) for i in range(devices)])


def to_odd(x, devices):
    return lax.ppermute(x, AXES, [(i, i + 1) for i in range(0, devices, 2)])


def to_even(x, devices):
    return lax.ppermute(x, AXES, [(i + 1, i) for i in range(0, devices, 2)])


def after(x, *others):
    return lax.optimization_barrier((x, *others))[0]


def dot_rows(left, right):
    return lax.dot_general(
        left, right, (((1,), (1,)), ((), ())), preferred_element_type=jnp.float32
    )


def dot_cols(left, right):
    return lax.dot_general(
        left, right, (((0,), (0,)), ((), ())), preferred_element_type=jnp.float32
    )


def dot(left, right):
    return jnp.dot(left, right, preferred_element_type=jnp.float32)


def merged(x, unit, pick_ref, at):
    if at >= unit:
        return x[at : at + STRIP]
    last = x.shape[0] - unit + at
    own = pick_ref[at : at + STRIP] > 0.5
    return jnp.where(own, x[last : last + STRIP], x[at : at + STRIP])


def spread(strips, unit, tri):
    edge = jnp.concatenate(strips[: unit // STRIP], axis=0)
    own = edge * tri
    return jnp.concatenate([edge - own] + strips[unit // STRIP :] + [own], axis=0)


def weigh(scores, dprobs, unit, bounds, pick_ref, tri):
    strips = range(0, scores.shape[0] - unit, STRIP)
    kept, peak = [], None
    for at in strips:
        s = jnp.minimum(merged(scores, unit, pick_ref, at), bounds[at : at + STRIP])
        kept.append(s)
        peak = s if peak is None else jnp.maximum(peak, s)
    peak = jnp.max(peak, axis=0, keepdims=True)
    low, dps = [], []
    total, weighted = 0.0, 0.0
    for at, s in zip(strips, kept):
        e = jnp.exp2((s - peak) * log2_scale)
        dp = merged(dprobs, unit, pick_ref, at)
        total = total + e
        weighted = weighted + e * dp
        low.append(e.astype(jnp.bfloat16))
        dps.append(dp)
    inverse = 1.0 / jnp.sum(total, axis=0, keepdims=True)
    delta = jnp.sum(weighted, axis=0, keepdims=True) * inverse
    ds = [e * (dp - delta).astype(jnp.bfloat16) for e, dp in zip(low, dps)]
    return spread(low, unit, tri), spread(ds, unit, tri), inverse


def products(q, g, k, low, ds, inverse):
    by_row = jnp.transpose(jnp.broadcast_to(inverse, (HEAD_SIZE, q.shape[0])))
    g_scaled = (g.astype(jnp.float32) * by_row).astype(jnp.bfloat16)
    q_scaled = (q.astype(jnp.float32) * (by_row * scale_factor)).astype(jnp.bfloat16)
    dv = dot(low, g_scaled)
    dk = dot(ds, q_scaled)
    dq = jnp.transpose(dot_cols(k, ds) * (inverse * scale_factor)).astype(jnp.bfloat16)
    return dq, dk, dv


def kernel(rows, back, group, split, pieces, starts_ref, q_ref, g_ref, k_ref, v_ref, *refs):
    pairs = [refs[2 * j : 2 * j + 2] for j in range(back + split)]
    outs = refs[len(refs) - (back + 1 + pieces) - 3 : len(refs) - 3]
    bound_ref, pick_ref, tri_ref = refs[-3:]
    dq_ref, own_ref, near_refs, far_refs = outs[0], outs[1], outs[2 : 2 + pieces], outs[2 + pieces :]
    unit = min(UNIT, rows)
    units = rows // unit
    columns = group * unit
    span = back * rows

    @pl.when(pl.program_id(0) == 0)
    def _():
        col = lax.broadcasted_iota(jnp.int32, (unit, columns), 1) % unit
        row = lax.broadcasted_iota(jnp.int32, (unit, columns), 0)
        own = row <= col
        pick_ref[...] = own.astype(jnp.float32)
        tri_ref[...] = pick_ref[...].astype(jnp.bfloat16)
        for u in range(units):
            base = device_index() * rows + u * unit
            pos = base + col[:1]
            start = jnp.zeros_like(pos)
            for doc in range(starts_ref.shape[0]):
                at = starts_ref[doc]
                start = jnp.where(pos >= at, at, start)
            start = jnp.broadcast_to(start, (unit, columns))
            for at in range(0, span, unit):
                key_pos = base - span + at + row
                if at == 0:
                    key_pos = jnp.where(own, key_pos + span, key_pos)
                bound_ref[u, at : at + unit] = jnp.where(key_pos >= start, jnp.inf, negative)

    tri = tri_ref[...]
    heads = range(k_ref.shape[1] // HEAD_SIZE)
    works = []
    for h in heads:
        at = slice(h * HEAD_SIZE, (h + 1) * HEAD_SIZE)

        def gathered(own, half):
            blocks = [pair[half][:, at] for pair in pairs]
            if split:
                blocks[:2] = [blocks[0] + blocks[1]]
            return jnp.concatenate(blocks[::-1] + [own[:, at]], axis=0)

        k_all = gathered(k_ref, 0)
        v_all = gathered(v_ref, 1)
        for u in range(units):
            of_rows = slice(u * unit, (u + 1) * unit)
            wide = [
                slice((h * group + m) * HEAD_SIZE, (h * group + m + 1) * HEAD_SIZE)
                for m in range(group)
            ]
            q = jnp.concatenate([q_ref[of_rows, w] for w in wide], axis=0)
            g = jnp.concatenate([g_ref[of_rows, w] for w in wide], axis=0)
            seen = slice(u * unit, u * unit + span + unit)
            works.append((h, u, of_rows, wide, q, g, k_all[seen], v_all[seen]))

    def begin(work):
        h, u, of_rows, wide, q, g, k, v = work
        return dot_rows(k, q), dot_rows(v, g)

    sums = {}
    ahead = begin(works[0])
    for i, work in enumerate(works):
        h, u, of_rows, wide, q, g, k, v = work
        scores, dprobs = ahead
        if i + 1 < len(works):
            ahead = begin(works[i + 1])
        low, ds, inverse = weigh(scores, dprobs, unit, bound_ref.at[u], pick_ref, tri)
        dq, dk, dv = products(q, g, k, low, ds, inverse)
        for m, w in enumerate(wide):
            dq_ref[of_rows, w] = dq[m * unit : (m + 1) * unit]
        for name, term in (("k", dk), ("v", dv)):
            for j in range((span + unit) // unit):
                key = (name, u + j)
                piece = term[j * unit : (j + 1) * unit]
                sums[key] = piece if key not in sums else sums[key] + piece
        if u + 1 < units:
            continue
        at = slice(h * HEAD_SIZE, (h + 1) * HEAD_SIZE)
        order = [[x] for x in far_refs[::-1]] + [near_refs, [own_ref]]
        for j, arrays in enumerate(order):
            height = 2 * rows // len(arrays)
            for name, below in (("k", 0), ("v", rows)):
                for of_unit in range(units):
                    piece, to = divmod(below + of_unit * unit, height)
                    total = sums[(name, j * units + of_unit)].astype(jnp.bfloat16)
                    arrays[piece][to : to + unit, at] = total
        sums = {}


def attend(
    doc_starts, queries, dout, keys, values, near, others, first, heads, buffer, pieces
):
    rows, width = keys.shape
    back = 1 + len(others)
    group = queries.shape[1] // width
    step = STEP * HEAD_SIZE
    unit = min(UNIT, rows)

    def part(height, wide, offset, row=0):
        return pl.BlockSpec((height, wide), lambda i: (row, offset // STEP + i))

    wide = part(rows, group * step, first)
    narrow = part(rows, step, first)
    smem = pl.BlockSpec(memory_space=pltpu.SMEM)
    operands = [doc_starts, queries, dout, keys, values]
    in_specs = [smem, wide, wide, narrow, narrow]
    for pair in near + others:
        operands += [pair[0], pair[-1]]
        in_specs += [part(rows, step, 0), part(rows, step, 0, 2 - len(pair))]
    if len(near) == 2:
        operands[5:] = [pltpu.with_memory_space_constraint(x, pltpu.VMEM) for x in operands[5:]]
    aliases = {}
    if buffer is not None:
        aliases = {len(operands): 0}
        operands.append(buffer)
        in_specs.append(pl.BlockSpec(memory_space=pl.ANY))
    whole = (2 * rows, heads * HEAD_SIZE)
    outs = [whole] + [(2 * rows // pieces, heads * HEAD_SIZE)] * pieces + [whole] * (back - 1)
    outs = [queries.shape] + outs
    return pl.pallas_call(
        functools.partial(kernel, rows, back, group, len(near) == 2, pieces),
        grid=(heads // STEP,),
        in_specs=in_specs,
        out_specs=[wide] + [part(shape[0], step, 0) for shape in outs[1:]],
        out_shape=[jax.ShapeDtypeStruct(outs[0], jnp.bfloat16)]
        + [pltpu.VMEM(shape, jnp.bfloat16) for shape in outs[1:]],
        scratch_shapes=[
            pltpu.VMEM((rows // unit, back * rows, group * unit), jnp.float32),
            pltpu.VMEM((unit, group * unit), jnp.float32),
            pltpu.VMEM((unit, group * unit), jnp.bfloat16),
        ],
        input_output_aliases=aliases,
        compiler_params=pltpu.CompilerParams(vmem_limit_bytes=VMEM_LIMIT),
        cost_estimate=pl.CostEstimate(flops=1, bytes_accessed=1, transcendentals=0),
        name="attend",
    )(*operands)


def pack_kernel(first, k_ref, v_ref, *refs):
    outs, sems = refs[:-1], refs[-1]
    rows, wide = k_ref.shape[0], outs[0].shape[1]
    columns = pl.ds(first * HEAD_SIZE, wide)
    copies = []
    for i, ref in enumerate((k_ref, v_ref)):
        place = outs[i] if len(outs) == 2 else outs[0].at[pl.ds(i * rows, rows)]
        copies.append(pltpu.make_async_copy(ref.at[:, columns], place, sems.at[i]))
        copies[-1].start()
    for copy in copies:
        copy.wait()


def pack(keys, values, first, heads, arrays):
    rows, wide = keys.shape[0], heads * HEAD_SIZE
    keys, values = (pltpu.with_memory_space_constraint(x, pltpu.HBM) for x in (keys, values))
    shape = (2 * rows // arrays, wide)
    return pl.pallas_call(
        functools.partial(pack_kernel, first),
        in_specs=[pl.BlockSpec(memory_space=pl.ANY)] * 2,
        out_specs=[pl.BlockSpec(memory_space=pltpu.VMEM)] * arrays,
        out_shape=[pltpu.VMEM(shape, keys.dtype)] * arrays,
        scratch_shapes=[pltpu.SemaphoreType.DMA((2,))],
        compiler_params=pltpu.CompilerParams(vmem_limit_bytes=4 * 1024 * 1024),
        name="pack",
    )(keys, values)


SMALL = pltpu.CompilerParams(vmem_limit_bytes=6 * 1024 * 1024)
FREE = pl.CostEstimate(flops=1, bytes_accessed=1, transcendentals=0)


def in_vmem(*arrays):
    return [pltpu.with_memory_space_constraint(x, pltpu.VMEM) for x in arrays]


def merge_kernel(far_ref, back_ref, out_ref):
    odd = device_index() % 2 == 1

    @pl.when(odd)
    def _():
        out_ref[...] = (
            far_ref[...].astype(jnp.float32) + back_ref[...].astype(jnp.float32)
        ).astype(out_ref.dtype)

    @pl.when(jnp.logical_not(odd))
    def _():
        out_ref[...] = far_ref[...]


def merge(far, back):
    whole = pl.BlockSpec(memory_space=pltpu.VMEM)
    return pl.pallas_call(
        merge_kernel,
        in_specs=[whole] * 2,
        out_specs=whole,
        out_shape=pltpu.VMEM(far.shape, far.dtype),
        compiler_params=SMALL,
        cost_estimate=FREE,
        name="merge",
    )(*in_vmem(far, back))


def merge_kept_kernel(far_ref, own_ref, back_ref, send_ref, kept_ref):
    odd = device_index() % 2 == 1

    @pl.when(odd)
    def _():
        total = far_ref[...].astype(jnp.float32) + back_ref[...].astype(jnp.float32)
        send_ref[...] = total.astype(send_ref.dtype)
        kept_ref[...] = own_ref[...]

    @pl.when(jnp.logical_not(odd))
    def _():
        send_ref[...] = far_ref[...]
        total = own_ref[...].astype(jnp.float32) + back_ref[...].astype(jnp.float32)
        kept_ref[...] = total.astype(kept_ref.dtype)


def merge_kept(far, own, back):
    whole = pl.BlockSpec(memory_space=pltpu.VMEM)
    return pl.pallas_call(
        merge_kept_kernel,
        in_specs=[whole] * 3,
        out_specs=[whole] * 2,
        out_shape=[pltpu.VMEM(far.shape, far.dtype)] * 2,
        compiler_params=SMALL,
        cost_estimate=FREE,
        name="merge_kept",
    )(*in_vmem(far, own, back))


def finish_kernel(first, terms, own_ref, home_ref, *refs):
    outs, total_ref, sems = refs[-4:-2], refs[-2], refs[-1]
    rows, wide = own_ref.shape[0] // 2, own_ref.shape[1]
    share = (1 - device_index() % 2).astype(jnp.float32)
    copies = []
    for i, out in enumerate(outs):
        half = slice(i * rows, (i + 1) * rows)
        total = own_ref[half].astype(jnp.float32) + home_ref[half].astype(jnp.float32)
        if terms == 3:
            total = total + share * refs[0][half].astype(jnp.float32)
        total_ref[half] = total.astype(total_ref.dtype)
        place = out.at[:, pl.ds(first * HEAD_SIZE, wide)]
        copies.append(pltpu.make_async_copy(total_ref.at[half], place, sems.at[i]))
        copies[-1].start()
    for copy in copies:
        copy.wait()


def finish(own, home, back, first, width, buffers):
    whole = pl.BlockSpec(memory_space=pltpu.VMEM)
    anywhere = pl.BlockSpec(memory_space=pl.ANY)
    operands = in_vmem(own, home, *back)
    terms = len(operands)
    in_specs = [whole] * terms
    aliases = {}
    if buffers is not None:
        aliases = {terms: 0, terms + 1: 1}
        operands += buffers
        in_specs += [anywhere] * 2
    return pl.pallas_call(
        functools.partial(finish_kernel, first, terms),
        in_specs=in_specs,
        out_specs=[anywhere] * 2,
        out_shape=[pltpu.HBM((own.shape[0] // 2, width), own.dtype)] * 2,
        scratch_shapes=[pltpu.VMEM(own.shape, own.dtype), pltpu.SemaphoreType.DMA((2,))],
        input_output_aliases=aliases,
        compiler_params=SMALL,
        cost_estimate=FREE,
        name="finish",
    )(*operands)


def shards(queries, keys, values, dout, doc_starts):
    rows, width = keys.shape
    kv_heads = width // HEAD_SIZE
    back = WINDOW_LENGTH // rows
    devices = lax.axis_size("seq") * lax.axis_size("head")
    if back != 2 or lax.axis_size("head") % 2 != 0:
        both = jnp.concatenate([keys, values], axis=0)
        halos = [shifted(both, j, devices) for j in range(1, back + 1)]
        dquery, own, *sent = attend(
            doc_starts, queries, dout, keys, values, [[halos[0]]], [[x] for x in halos[1:]], 0,
            kv_heads, None, 1,
        )
        total = own.astype(jnp.float32)
        for j in range(back):
            total = total + shifted(sent[j], -(j + 1), devices).astype(jnp.float32)
        total = total.astype(jnp.bfloat16)
        return (dquery, total[:rows], total[rows:])

    starts = [sum(GROUPS[:c]) for c in range(len(GROUPS))]
    packed = [pack(keys, values, start, heads, 1)[0] for start, heads in zip(starts, GROUPS)]
    far = [shifted(x, 2, devices) for x in packed]
    early = [to_odd(x, devices) for x in packed]

    def work(start, heads, received, own_near, dquery):
        near = to_even(received, devices)
        dquery, own, to_near, to_far = attend(
            doc_starts, queries, dout, keys, values, [[near], [own_near]], [[received]],
            start, heads, dquery, 1,
        )
        returned = swapped(to_near, devices)
        if start == starts[-1]:
            return dquery, *merge_kept(to_far, own, returned)
        return dquery, merge(to_far, returned), own, returned

    always = (doc_starts[0] | 1) != 0
    dquery, homes, kept = None, [], []
    for start, heads, received, own_near in zip(starts, GROUPS, far, early):
        def skip(received, own_near, dquery):
            zeros = jnp.zeros_like(received)
            parts = [zeros] * (2 if start == starts[-1] else 3)
            return jnp.zeros_like(queries) if dquery is None else dquery, *parts

        dquery, send, own, *returned = lax.cond(
            always, functools.partial(work, start, heads), skip, received, own_near, dquery
        )
        homes.append(shifted(send, -2, devices))
        kept.append((own, returned))
    grads = None
    for start, home, (own, returned) in zip(starts, homes, kept):
        grads = finish(own, home, returned, start, width, grads)
    dkey, dvalue = grads
    return (dquery, dkey, dvalue)


def solution(mesh):
    spec = P(AXES, None)
    return jax.shard_map(
        shards,
        mesh=mesh,
        in_specs=(spec, spec, spec, spec, P()),
        out_specs=(spec, spec, spec),
        check_vma=False,
    )
```

```python
import functools
import math

import jax
import jax.numpy as jnp
from jax import lax
from jax.experimental import pallas as pl
from jax.experimental.pallas import tpu as pltpu
from jax.sharding import PartitionSpec as P

HEAD_SIZE = 128
WINDOW_LENGTH = 512
AXES = ("seq", "head")
GROUPS = (6, 6, 4)
STEP = 2
LAST_STEP = 4
UNIT = 128
STRIP = 32
VMEM_LIMIT = 16 * 1024 * 1024


scale_factor = 168.0 ** (-0.5)
log2_scale = scale_factor * math.log2(math.e)
negative = -1e30


def device_index():
    return lax.axis_index("seq") * lax.axis_size("head") + lax.axis_index("head")


def shifted(x, by, devices):
    pairs = [(i, i + by) for i in range(devices) if 0 <= i + by < devices]
    return lax.ppermute(x, AXES, pairs)


def swapped(x, devices):
    return lax.ppermute(x, AXES, [(i, i ^ 1) for i in range(devices)])


def to_odd(x, devices):
    return lax.ppermute(x, AXES, [(i, i + 1) for i in range(0, devices, 2)])


def to_even(x, devices):
    return lax.ppermute(x, AXES, [(i + 1, i) for i in range(0, devices, 2)])


def after(x, *others):
    return lax.optimization_barrier((x, *others))[0]


def dot_rows(left, right):
    return lax.dot_general(
        left, right, (((1,), (1,)), ((), ())), preferred_element_type=jnp.float32
    )


def dot_cols(left, right):
    return lax.dot_general(
        left, right, (((0,), (0,)), ((), ())), preferred_element_type=jnp.float32
    )


def dot(left, right):
    return jnp.dot(left, right, preferred_element_type=jnp.float32)


def merged(x, unit, pick_ref, at):
    if at >= unit:
        return x[at : at + STRIP]
    last = x.shape[0] - unit + at
    own = pick_ref[at : at + STRIP] > 0.5
    return jnp.where(own, x[last : last + STRIP], x[at : at + STRIP])


def spread(strips, unit, tri):
    edge = jnp.concatenate(strips[: unit // STRIP], axis=0)
    own = edge * tri
    return jnp.concatenate([edge - own] + strips[unit // STRIP :] + [own], axis=0)


def weigh(scores, dprobs, unit, bounds, pick_ref, tri):
    strips = range(0, scores.shape[0] - unit, STRIP)
    kept, peak = [], None
    for at in strips:
        s = jnp.minimum(merged(scores, unit, pick_ref, at), bounds[at : at + STRIP])
        kept.append(s)
        peak = s if peak is None else jnp.maximum(peak, s)
    peak = jnp.max(peak, axis=0, keepdims=True)
    low, dps = [], []
    total, weighted = 0.0, 0.0
    for at, s in zip(strips, kept):
        e = jnp.exp2((s - peak) * log2_scale)
        dp = merged(dprobs, unit, pick_ref, at)
        total = total + e
        weighted = weighted + e * dp
        low.append(e.astype(jnp.bfloat16))
        dps.append(dp)
    inverse = 1.0 / jnp.sum(total, axis=0, keepdims=True)
    delta = jnp.sum(weighted, axis=0, keepdims=True) * inverse
    ds = [e * (dp - delta).astype(jnp.bfloat16) for e, dp in zip(low, dps)]
    return spread(low, unit, tri), spread(ds, unit, tri), inverse


def products(q, g, k, low, ds, inverse):
    by_row = jnp.transpose(jnp.broadcast_to(inverse, (HEAD_SIZE, q.shape[0])))
    g_scaled = (g.astype(jnp.float32) * by_row).astype(jnp.bfloat16)
    q_scaled = (q.astype(jnp.float32) * (by_row * scale_factor)).astype(jnp.bfloat16)
    dv = dot(low, g_scaled)
    dk = dot(ds, q_scaled)
    dq = jnp.transpose(dot_cols(k, ds) * (inverse * scale_factor)).astype(jnp.bfloat16)
    return dq, dk, dv


def kernel(rows, back, group, split, pieces, starts_ref, q_ref, g_ref, k_ref, v_ref, *refs):
    pairs = [refs[2 * j : 2 * j + 2] for j in range(back + split)]
    outs = refs[len(refs) - (back + 1 + pieces) - 3 : len(refs) - 3]
    bound_ref, pick_ref, tri_ref = refs[-3:]
    dq_ref, own_ref, near_refs, far_refs = outs[0], outs[1], outs[2 : 2 + pieces], outs[2 + pieces :]
    unit = min(UNIT, rows)
    units = rows // unit
    columns = group * unit
    span = back * rows

    @pl.when(pl.program_id(0) == 0)
    def _():
        col = lax.broadcasted_iota(jnp.int32, (unit, columns), 1) % unit
        row = lax.broadcasted_iota(jnp.int32, (unit, columns), 0)
        own = row <= col
        pick_ref[...] = own.astype(jnp.float32)
        tri_ref[...] = pick_ref[...].astype(jnp.bfloat16)
        for u in range(units):
            base = device_index() * rows + u * unit
            pos = base + col[:1]
            start = jnp.zeros_like(pos)
            for doc in range(starts_ref.shape[0]):
                at = starts_ref[doc]
                start = jnp.where(pos >= at, at, start)
            start = jnp.broadcast_to(start, (unit, columns))
            for at in range(0, span, unit):
                key_pos = base - span + at + row
                if at == 0:
                    key_pos = jnp.where(own, key_pos + span, key_pos)
                bound_ref[u, at : at + unit] = jnp.where(key_pos >= start, jnp.inf, negative)

    tri = tri_ref[...]
    heads = range(k_ref.shape[1] // HEAD_SIZE)
    works = []
    for h in heads:
        at = slice(h * HEAD_SIZE, (h + 1) * HEAD_SIZE)

        def gathered(own, half):
            blocks = [pair[half][:, at] for pair in pairs]
            if split:
                blocks[:2] = [blocks[0] + blocks[1]]
            return jnp.concatenate(blocks[::-1] + [own[:, at]], axis=0)

        k_all = gathered(k_ref, 0)
        v_all = gathered(v_ref, 1)
        for u in range(units):
            of_rows = slice(u * unit, (u + 1) * unit)
            wide = [
                slice((h * group + m) * HEAD_SIZE, (h * group + m + 1) * HEAD_SIZE)
                for m in range(group)
            ]
            q = jnp.concatenate([q_ref[of_rows, w] for w in wide], axis=0)
            g = jnp.concatenate([g_ref[of_rows, w] for w in wide], axis=0)
            seen = slice(u * unit, u * unit + span + unit)
            works.append((h, u, of_rows, wide, q, g, k_all[seen], v_all[seen]))

    def begin(work):
        h, u, of_rows, wide, q, g, k, v = work
        return dot_rows(k, q), dot_rows(v, g)

    sums = {}
    ahead = begin(works[0])
    for i, work in enumerate(works):
        h, u, of_rows, wide, q, g, k, v = work
        scores, dprobs = ahead
        if i + 1 < len(works):
            ahead = begin(works[i + 1])
        low, ds, inverse = weigh(scores, dprobs, unit, bound_ref.at[u], pick_ref, tri)
        dq, dk, dv = products(q, g, k, low, ds, inverse)
        for m, w in enumerate(wide):
            dq_ref[of_rows, w] = dq[m * unit : (m + 1) * unit]
        for name, term in (("k", dk), ("v", dv)):
            for j in range((span + unit) // unit):
                key = (name, u + j)
                piece = term[j * unit : (j + 1) * unit]
                sums[key] = piece if key not in sums else sums[key] + piece
        if u + 1 < units:
            continue
        at = slice(h * HEAD_SIZE, (h + 1) * HEAD_SIZE)
        order = [[x] for x in far_refs[::-1]] + [near_refs, [own_ref]]
        for j, arrays in enumerate(order):
            height = 2 * rows // len(arrays)
            for name, below in (("k", 0), ("v", rows)):
                for of_unit in range(units):
                    piece, to = divmod(below + of_unit * unit, height)
                    total = sums[(name, j * units + of_unit)].astype(jnp.bfloat16)
                    arrays[piece][to : to + unit, at] = total
        sums = {}


def attend(
    doc_starts, queries, dout, keys, values, near, others, first, heads, buffer, pieces
):
    rows, width = keys.shape
    back = 1 + len(others)
    group = queries.shape[1] // width
    each = LAST_STEP if heads == LAST_STEP else STEP
    step = each * HEAD_SIZE
    unit = min(UNIT, rows)

    def part(height, wide, offset, row=0):
        return pl.BlockSpec((height, wide), lambda i: (row, offset // each + i))

    wide = part(rows, group * step, first)
    narrow = part(rows, step, first)
    smem = pl.BlockSpec(memory_space=pltpu.SMEM)
    operands = [doc_starts, queries, dout, keys, values]
    in_specs = [smem, wide, wide, narrow, narrow]
    for pair in near + others:
        operands += [pair[0], pair[-1]]
        in_specs += [part(rows, step, 0), part(rows, step, 0, 2 - len(pair))]
    if len(near) == 2:
        operands[5:] = [pltpu.with_memory_space_constraint(x, pltpu.VMEM) for x in operands[5:]]
    aliases = {}
    if buffer is not None:
        aliases = {len(operands): 0}
        operands.append(buffer)
        in_specs.append(pl.BlockSpec(memory_space=pl.ANY))
    whole = (2 * rows, heads * HEAD_SIZE)
    outs = [whole] + [(2 * rows // pieces, heads * HEAD_SIZE)] * pieces + [whole] * (back - 1)
    outs = [queries.shape] + outs
    return pl.pallas_call(
        functools.partial(kernel, rows, back, group, len(near) == 2, pieces),
        grid=(heads // each,),
        in_specs=in_specs,
        out_specs=[wide] + [part(shape[0], step, 0) for shape in outs[1:]],
        out_shape=[jax.ShapeDtypeStruct(outs[0], jnp.bfloat16)]
        + [pltpu.VMEM(shape, jnp.bfloat16) for shape in outs[1:]],
        scratch_shapes=[
            pltpu.VMEM((rows // unit, back * rows, group * unit), jnp.float32),
            pltpu.VMEM((unit, group * unit), jnp.float32),
            pltpu.VMEM((unit, group * unit), jnp.bfloat16),
        ],
        input_output_aliases=aliases,
        compiler_params=pltpu.CompilerParams(vmem_limit_bytes=VMEM_LIMIT),
        cost_estimate=pl.CostEstimate(flops=1, bytes_accessed=1, transcendentals=0),
        name="attend",
    )(*operands)


def pack_kernel(first, k_ref, v_ref, *refs):
    outs, sems = refs[:-1], refs[-1]
    rows, wide = k_ref.shape[0], outs[0].shape[1]
    columns = pl.ds(first * HEAD_SIZE, wide)
    copies = []
    for i, ref in enumerate((k_ref, v_ref)):
        place = outs[i] if len(outs) == 2 else outs[0].at[pl.ds(i * rows, rows)]
        copies.append(pltpu.make_async_copy(ref.at[:, columns], place, sems.at[i]))
        copies[-1].start()
    for copy in copies:
        copy.wait()


def pack(keys, values, first, heads, arrays):
    rows, wide = keys.shape[0], heads * HEAD_SIZE
    keys, values = (pltpu.with_memory_space_constraint(x, pltpu.HBM) for x in (keys, values))
    shape = (2 * rows // arrays, wide)
    return pl.pallas_call(
        functools.partial(pack_kernel, first),
        in_specs=[pl.BlockSpec(memory_space=pl.ANY)] * 2,
        out_specs=[pl.BlockSpec(memory_space=pltpu.VMEM)] * arrays,
        out_shape=[pltpu.VMEM(shape, keys.dtype)] * arrays,
        scratch_shapes=[pltpu.SemaphoreType.DMA((2,))],
        compiler_params=pltpu.CompilerParams(vmem_limit_bytes=4 * 1024 * 1024),
        name="pack",
    )(keys, values)


SMALL = pltpu.CompilerParams(vmem_limit_bytes=6 * 1024 * 1024)
FREE = pl.CostEstimate(flops=1, bytes_accessed=1, transcendentals=0)


def in_vmem(*arrays):
    return [pltpu.with_memory_space_constraint(x, pltpu.VMEM) for x in arrays]


def merge_kernel(far_ref, back_ref, out_ref):
    odd = device_index() % 2 == 1

    @pl.when(odd)
    def _():
        out_ref[...] = (
            far_ref[...].astype(jnp.float32) + back_ref[...].astype(jnp.float32)
        ).astype(out_ref.dtype)

    @pl.when(jnp.logical_not(odd))
    def _():
        out_ref[...] = far_ref[...]


def merge(far, back):
    whole = pl.BlockSpec(memory_space=pltpu.VMEM)
    return pl.pallas_call(
        merge_kernel,
        in_specs=[whole] * 2,
        out_specs=whole,
        out_shape=pltpu.VMEM(far.shape, far.dtype),
        compiler_params=SMALL,
        cost_estimate=FREE,
        name="merge",
    )(*in_vmem(far, back))


def merge_kept_kernel(far_ref, own_ref, back_ref, send_ref, kept_ref):
    odd = device_index() % 2 == 1

    @pl.when(odd)
    def _():
        total = far_ref[...].astype(jnp.float32) + back_ref[...].astype(jnp.float32)
        send_ref[...] = total.astype(send_ref.dtype)
        kept_ref[...] = own_ref[...]

    @pl.when(jnp.logical_not(odd))
    def _():
        send_ref[...] = far_ref[...]
        total = own_ref[...].astype(jnp.float32) + back_ref[...].astype(jnp.float32)
        kept_ref[...] = total.astype(kept_ref.dtype)


def merge_kept(far, own, back):
    whole = pl.BlockSpec(memory_space=pltpu.VMEM)
    return pl.pallas_call(
        merge_kept_kernel,
        in_specs=[whole] * 3,
        out_specs=[whole] * 2,
        out_shape=[pltpu.VMEM(far.shape, far.dtype)] * 2,
        compiler_params=SMALL,
        cost_estimate=FREE,
        name="merge_kept",
    )(*in_vmem(far, own, back))


def finish_kernel(first, terms, own_ref, home_ref, *refs):
    outs, total_ref, sems = refs[-4:-2], refs[-2], refs[-1]
    rows, wide = own_ref.shape[0] // 2, own_ref.shape[1]
    share = (1 - device_index() % 2).astype(jnp.float32)
    copies = []
    for i, out in enumerate(outs):
        half = slice(i * rows, (i + 1) * rows)
        total = own_ref[half].astype(jnp.float32) + home_ref[half].astype(jnp.float32)
        if terms == 3:
            total = total + share * refs[0][half].astype(jnp.float32)
        total_ref[half] = total.astype(total_ref.dtype)
        place = out.at[:, pl.ds(first * HEAD_SIZE, wide)]
        copies.append(pltpu.make_async_copy(total_ref.at[half], place, sems.at[i]))
        copies[-1].start()
    for copy in copies:
        copy.wait()


def finish(own, home, back, first, width, buffers):
    whole = pl.BlockSpec(memory_space=pltpu.VMEM)
    anywhere = pl.BlockSpec(memory_space=pl.ANY)
    operands = in_vmem(own, home, *back)
    terms = len(operands)
    in_specs = [whole] * terms
    aliases = {}
    if buffers is not None:
        aliases = {terms: 0, terms + 1: 1}
        operands += buffers
        in_specs += [anywhere] * 2
    return pl.pallas_call(
        functools.partial(finish_kernel, first, terms),
        in_specs=in_specs,
        out_specs=[anywhere] * 2,
        out_shape=[pltpu.HBM((own.shape[0] // 2, width), own.dtype)] * 2,
        scratch_shapes=[pltpu.VMEM(own.shape, own.dtype), pltpu.SemaphoreType.DMA((2,))],
        input_output_aliases=aliases,
        compiler_params=SMALL,
        cost_estimate=FREE,
        name="finish",
    )(*operands)


def shards(queries, keys, values, dout, doc_starts):
    rows, width = keys.shape
    kv_heads = width // HEAD_SIZE
    back = WINDOW_LENGTH // rows
    devices = lax.axis_size("seq") * lax.axis_size("head")
    if back != 2 or lax.axis_size("head") % 2 != 0:
        both = jnp.concatenate([keys, values], axis=0)
        halos = [shifted(both, j, devices) for j in range(1, back + 1)]
        dquery, own, *sent = attend(
            doc_starts, queries, dout, keys, values, [[halos[0]]], [[x] for x in halos[1:]], 0,
            kv_heads, None, 1,
        )
        total = own.astype(jnp.float32)
        for j in range(back):
            total = total + shifted(sent[j], -(j + 1), devices).astype(jnp.float32)
        total = total.astype(jnp.bfloat16)
        return (dquery, total[:rows], total[rows:])

    starts = [sum(GROUPS[:c]) for c in range(len(GROUPS))]
    packed = [pack(keys, values, start, heads, 1)[0] for start, heads in zip(starts, GROUPS)]
    far = [shifted(x, 2, devices) for x in packed]
    early = [to_odd(x, devices) for x in packed]

    def work(start, heads, received, own_near, dquery):
        near = to_even(received, devices)
        dquery, own, to_near, to_far = attend(
            doc_starts, queries, dout, keys, values, [[near], [own_near]], [[received]],
            start, heads, dquery, 1,
        )
        returned = swapped(to_near, devices)
        if start > 0:
            return dquery, *merge_kept(to_far, own, returned)
        return dquery, merge(to_far, returned), own, returned

    always = (doc_starts[0] | 1) != 0
    dquery, homes, kept = None, [], []
    for start, heads, received, own_near in zip(starts, GROUPS, far, early):
        def skip(received, own_near, dquery):
            zeros = jnp.zeros_like(received)
            parts = [zeros] * (2 if start > 0 else 3)
            return jnp.zeros_like(queries) if dquery is None else dquery, *parts

        dquery, send, own, *returned = lax.cond(
            always, functools.partial(work, start, heads), skip, received, own_near, dquery
        )
        homes.append(shifted(send, -2, devices))
        kept.append((own, returned))
    grads = None
    for start, home, (own, returned) in zip(starts, homes, kept):
        grads = finish(own, home, returned, start, width, grads)
    dkey, dvalue = grads
    return (dquery, dkey, dvalue)


def solution(mesh):
    spec = P(AXES, None)
    return jax.shard_map(
        shards,
        mesh=mesh,
        in_specs=(spec, spec, spec, spec, P()),
        out_specs=(spec, spec, spec),
        check_vma=False,
    )
```
